32 devices in a mesh: rep: 4 (over y, x), seq: 4 (over z), shard: 2 (over core).
Axes of the slice: x: 2, y: 2, z: 4, core: 2. Of those that a mesh axis runs over, the one named last changes fastest.
Arguments:
- tokens: bfloat16 [8, 1024, 768], P(('rep', 'shard'), 'seq'), may hold values from -6 to 6
- out_grad: bfloat16 [8, 1024, 768], P(('rep', 'shard'), 'seq'), may hold values from -6 to 6
- attention_gain: bfloat16 [768], P(('seq', 'shard')), may hold values from 0.099609375 to 1.8984375
- query_weight: bfloat16 [768, 768], P(('seq', 'shard')), may hold values from -0.02734375 to 0.02734375
- key_weight: bfloat16 [768, 768], P(('seq', 'shard')), may hold values from -0.21875 to 0.21875
- value_weight: bfloat16 [768, 768], P(('seq', 'shard')), may hold values from -0.21875 to 0.21875
- output_weight: bfloat16 [768, 768], P(('seq', 'shard')), may hold values from -3.5 to 3.5
- position_bias: bfloat16 [384], P(('seq', 'shard')), may hold values from -4 to 4
- bucket_table: int32 [2047], replicated, may hold values from 0 to 31
- feedforward_gain: bfloat16 [768], P(('seq', 'shard')), may hold values from 0.099609375 to 1.8984375
- router_matrix: bfloat16 [768, 8], P(('seq', 'shard')), may hold values from -0.109375 to 0.109375
- routes: int32 [8, 1024, 1], P(('rep', 'shard'), 'seq'), may hold values from 0 to 7; in each aligned block of 256 rows (0 to 255, 256 to 511, ..., all dimensions but the last counted through in order) at most 64 rows name the same one
- up_weight: bfloat16 [8, 3072, 768], P(('seq', 'shard'), 'rep'), may hold values from -0.21875 to 0.21875
- down_weight: bfloat16 [8, 3072, 768], P(('seq', 'shard'), 'rep'), may hold values from -4 to 4
Outputs:
- layer_output: bfloat16 [8, 1024, 768], P(('rep', 'shard'), 'seq')
- token_input_gradient: float32 [8, 1024, 768], P(('rep', 'shard'), 'seq')
- attention_gain_grad: float32 [768], P(('seq', 'shard'))
- query_weight_grad: float32 [768, 768], P(('seq', 'shard'))
- key_weight_grad: float32 [768, 768], P(('seq', 'shard'))
- value_weight_grad: float32 [768, 768], P(('seq', 'shard'))
- output_weight_grad: float32 [768, 768], P(('seq', 'shard'))
- position_bias_grad: float32 [384], P(('seq', 'shard'))
- feedforward_gain_grad: float32 [768], P(('seq', 'shard'))
- router_weight_grad: float32 [768, 8], P(('seq', 'shard'))
- up_weight_grad: float32 [8, 3072, 768], P(('seq', 'shard'), 'rep')
- down_weight_grad: float32 [8, 3072, 768], P(('seq', 'shard'), 'rep')
The draws below stay inside these ranges and needn't reach their ends.
Inputs may be any that keep to these rules, and one draw needn't show every extreme that they name: `routes`: in each aligned block of 256 rows in sequence order (the rows of one device) no expert is named more than 64 times, a bound that some block reaches.
All inputs are finite; a program needn't handle non-finite values.
Results may differ from the reference program's by a relative error of at most 0.02.
Values may be sent and summed in bfloat16 or wider, within the bound.
No kernel may reach another device: no remote copies, remote signals or barrier semaphores. Data moves between devices by JAX's collectives and lax.ppermute only.
A program may use at most 128 MiB of HBM per device.

```python
import math
import jax
import jax.numpy as jnp
import numpy as np
from jax import lax

D = 768
HEADS = 12
FF = 3072
BUCKETS = 32
TOK_DEV = 256
HD = 64
LEN = 1024
SEQS = 8
EXPERTS = 8
CAP = 64


def touch_ends(drawn, stream_key, low, top_value):
    longest = drawn.shape.index(max(drawn.shape))
    spots = []
    for shift in (0, 1):
        where = [jax.random.randint(jax.random.fold_in(stream_key, axis), (), 0, length) for axis, length in enumerate(drawn.shape)]
        where[longest] = (where[longest] + shift) % drawn.shape[longest]
        spots.append(tuple(where))
    return drawn.at[spots[0]].set(low).at[spots[1]].set(top_value)


def shard_levels(own_key, shape, cuts, least, largest):
    loudness = 1.0
    for dim, shards_of in cuts:
        draws = jax.random.uniform(jax.random.fold_in(jax.random.fold_in(own_key, 6), dim), (shards_of,), jnp.float32, least / len(cuts), largest / len(cuts))
        loudness = loudness * jnp.repeat(jnp.exp(draws), shape[dim] // shards_of).reshape((-1,) + (1,) * (len(shape) - 1 - dim))
    return loudness


def routed_block(stream_key, own, number, rows, amount, top, most, skew):
    ranking = jax.random.permutation(stream_key, amount)
    crowded, common = portions_of(amount, rows * top, most, skew, True), portions_of(amount, rows * top, most, skew, False)
    places = jnp.arange(amount)

    def named(tallies, turn):
        used = int((tallies > 0).sum())
        fixed = max(1, used // 4)
        moved = fixed + (places - fixed + turn * (used - fixed)) % max(1, amount - fixed)
        return jnp.zeros((amount,), jnp.int32).at[ranking[jnp.where(places < fixed, places, moved)]].set(jnp.asarray(tallies, jnp.int32))

    tallies = jnp.where(number % 4 == 0, named(crowded, number // 4), named(common, number - number // 4 - 1))
    mixed = jax.random.permutation(jax.random.fold_in(own, 3), amount)
    source_of, receiver = mixed[0:amount // 2 * 2:2], mixed[1:amount // 2 * 2:2]
    room = jnp.minimum(tallies[source_of] - 1, most - tallies[receiver]) // 2
    room = jnp.where((source_of == ranking[0]) | (receiver == ranking[0]) | (tallies[receiver] == 0), 0, jnp.maximum(room, 0))
    moved = jax.random.randint(jax.random.fold_in(own, 4), (amount // 2,), 0, 1 << 20) % (room + 1)
    tallies = tallies.at[source_of].add(-moved).at[receiver].add(moved)
    members = jnp.searchsorted(jnp.cumsum(tallies), jnp.arange(rows * top), side="right").astype(jnp.int32)
    listing = members.reshape(top, rows).T
    listing = listing[jax.random.permutation(jax.random.fold_in(own, 1), rows)]
    turn = jax.random.randint(jax.random.fold_in(own, 2), (rows, 1), 0, top)
    return jnp.take_along_axis(listing, (jnp.arange(top)[None, :] + turn) % top, axis=1)


def portions_of(amount, total, most, skew, full):
    weights = [(1 << 20) // math.isqrt(grade ** skew) + 1 for grade in range(1, amount + 1)]
    largest = most if full else min(most, max(-(-total // amount), total * weights[0] // sum(weights)))
    least = 1 if total - largest >= amount - 1 else 0
    counts, spare = [largest] + [least] * (amount - 1), total - largest - least * (amount - 1)
    while spare > 0:
        free = [i for i in range(1, amount) if counts[i] < largest] or [i for i in range(1, amount) if counts[i] < most]
        mass, budget = sum([weights[i] for i in free]), spare
        for i in free:
            more = min(most - counts[i], max(1, budget * weights[i] // mass), spare)
            counts[i] = counts[i] + more
            spare = spare - more
    return np.array(counts)


def normal_values(rng, dims, spread, bound, pieces=(), held_as=jnp.bfloat16):
    array = spread * jax.random.normal(rng, dims, jnp.float32)
    if pieces:
        array = array * shard_levels(rng, dims, pieces, -0.22, 0.18)
    return jnp.clip(array, -bound, bound).astype(held_as)


def setup_inputs(seed: int = 0) -> dict:
    keys = jax.random.split(jax.random.key(seed), 15)
    tokens = normal_values(keys[0], (SEQS, LEN, D), 1.0, 6.0, ((0, 8), (1, 4)))
    out_grad = normal_values(keys[1], (SEQS, LEN, D), 1.0, 6.0, ((0, 8), (1, 4)))
    attention_gain = jnp.clip(1.0 + 0.18 * jax.random.normal(keys[2], (D,), jnp.float32), 0.099609375, 1.8984375).astype(jnp.bfloat16)
    query_weight = normal_values(keys[3], (D, D), (D * HD) ** -0.5, 0.02734375, ((0, 8),))
    key_weight = normal_values(keys[4], (D, D), D ** -0.5, 0.21875, ((0, 8),))
    value_weight = normal_values(keys[5], (D, D), D ** -0.5, 0.21875, ((0, 8),))
    output_weight = normal_values(keys[6], (D, D), (max(1, D * 4 // LEN)) ** -0.5, 3.5, ((0, 8),))
    position_bias = normal_values(keys[7], (BUCKETS * HEADS,), 1.0, 4.0, ((0, 8),))
    bucket_table = touch_ends(jax.random.randint(keys[8], (2 * LEN - 1,), 0, BUCKETS), jax.random.fold_in(keys[8], 1), 0, BUCKETS - 1).astype(jnp.int32)
    feedforward_gain = jnp.clip(1.0 + 0.18 * jax.random.normal(keys[9], (D,), jnp.float32), 0.099609375, 1.8984375).astype(jnp.bfloat16)
    router_matrix = normal_values(keys[10], (D, EXPERTS), (4 * D) ** -0.5, 0.109375, ((0, 8),))
    routes_keys = jax.random.split(jax.random.fold_in(keys[11], 1), SEQS * LEN // TOK_DEV)
    routes_turns = jax.random.permutation(jax.random.fold_in(keys[11], 3), SEQS * LEN // TOK_DEV)
    routes = jax.vmap(lambda own, number: routed_block(jax.random.fold_in(keys[11], 2), own, number, TOK_DEV, EXPERTS, 1, CAP, 1))(routes_keys, routes_turns).reshape((SEQS, LEN, 1))
    up_weight = normal_values(keys[12], (EXPERTS, FF, D), D ** -0.5, 0.21875, ((0, 8), (1, 4)))
    down_weight = normal_values(keys[13], (EXPERTS, FF, D), (2.0 * EXPERTS * FF ** -0.5), 4.0, ((0, 8), (1, 4)))
    return dict(tokens=tokens, out_grad=out_grad, attention_gain=attention_gain, query_weight=query_weight, key_weight=key_weight, value_weight=value_weight, output_weight=output_weight, position_bias=position_bias, bucket_table=bucket_table, feedforward_gain=feedforward_gain, router_matrix=router_matrix, routes=routes, up_weight=up_weight, down_weight=down_weight)


EPSILON = 1e-06
FULL_ACCURACY = lax.Precision.HIGHEST

@jax.custom_vjp
def low(v):
    return lax.optimization_barrier(v.astype(jnp.bfloat16)).astype(jnp.float32)

@jax.custom_vjp
def reduced_backward(v):
    return v

def low_keep(v):
    return (low(v), None)

def low_pass(kept, grad):
    return (grad,)

def back_keep(v):
    return (v, None)

def back_low(kept, grad):
    return (low(grad),)
low.defvjp(low_keep, low_pass)
reduced_backward.defvjp(back_keep, back_low)

def matmul(left, right):
    return jnp.dot(left, right, precision=FULL_ACCURACY, preferred_element_type=jnp.float32)

def rms_norm(values, gain_vec):
    return values * lax.rsqrt(lax.optimization_barrier(jnp.mean(values * values, axis=-1, keepdims=True)) + EPSILON) * gain_vec

def softmax_rows(scores):
    shifted = jnp.exp(scores - lax.optimization_barrier(jnp.max(scores, axis=-1, keepdims=True)))
    return shifted / lax.optimization_barrier(jnp.sum(shifted, axis=-1, keepdims=True))

def encoder_block_pass(tokens, attention_gain, query_weight, key_weight, value_weight, output_weight, position_bias, feedforward_gain, router_matrix, up_weight, down_weight, bucket_table, routes):
    length = tokens.shape[1]
    model_width = tokens.shape[2]
    head_count = position_bias.shape[0] // BUCKETS
    head_size = model_width // head_count
    experts = router_matrix.shape[1]
    bias_table = position_bias.reshape(BUCKETS, head_count)
    bucket_marks = (bucket_table[:, None] == jnp.arange(BUCKETS, dtype=jnp.int32)[None, :]).astype(jnp.float32)
    offset_bias = matmul(bucket_marks, bias_table)
    places = jnp.arange(length, dtype=jnp.int32)
    offsets = places[None, :] - places[:, None] + (length - 1)
    pos_bias = jnp.transpose(offset_bias[offsets], (2, 0, 1))

    def attend(row_block):
        normed = low(rms_norm(row_block, attention_gain))
        queries = low(reduced_backward(matmul(normed, query_weight))).reshape(length, head_count, head_size)
        key_rows = low(reduced_backward(matmul(normed, key_weight))).reshape(length, head_count, head_size)
        value_rows = low(reduced_backward(matmul(normed, value_weight))).reshape(length, head_count, head_size)
        scores = reduced_backward(jnp.einsum('ihd,jhd->hij', queries, key_rows, precision=FULL_ACCURACY) + pos_bias)
        attn_probs = low(softmax_rows(scores))
        context = jnp.einsum('hij,jhd->ihd', attn_probs, value_rows, precision=FULL_ACCURACY).reshape(length, model_width)
        context = low(reduced_backward(context))
        return row_block + reduced_backward(matmul(context, output_weight))
    middle = lax.map(jax.checkpoint(attend), tokens)
    normalized_feedforward = low(rms_norm(middle, feedforward_gain))
    router_logits = reduced_backward(jnp.einsum('ogt,tz->ogz', normalized_feedforward, router_matrix, precision=FULL_ACCURACY))
    router_probs = softmax_rows(router_logits)
    chosen = routes[..., 0]
    picked = (chosen[..., None] == jnp.arange(experts, dtype=jnp.int32)).astype(jnp.float32)
    gate_value = lax.optimization_barrier(jnp.sum(router_probs * picked, axis=-1, keepdims=True))
    blocks = chosen.reshape(-1, TOK_DEV)
    block_count = blocks.shape[0]
    block_marks = (blocks[..., None] == jnp.arange(experts, dtype=jnp.int32)).astype(jnp.int32)
    slot_ranks = lax.optimization_barrier(jnp.sum((jnp.cumsum(block_marks, axis=1) - block_marks) * block_marks, axis=-1))
    slot_index = (jnp.arange(block_count, dtype=jnp.int32)[:, None] * (experts * CAP) + blocks * CAP + slot_ranks).reshape(-1)
    sent_rows = reduced_backward(normalized_feedforward).reshape(-1, model_width)
    buffer = jnp.zeros((block_count * experts * CAP, model_width), jnp.float32).at[slot_index].set(sent_rows)
    grouped = buffer.reshape(block_count, experts, CAP, model_width).transpose(1, 0, 2, 3).reshape(experts, block_count * CAP, model_width)

    def expert(expert_parts):
        expert_rows, up_matrix, down_matrix = expert_parts
        pre_activation = reduced_backward(jnp.einsum('rd,fd->rf', expert_rows, up_matrix, precision=FULL_ACCURACY))
        hidden = low(jax.nn.gelu(pre_activation))
        return low(reduced_backward(matmul(hidden, down_matrix)))
    results = lax.map(jax.checkpoint(expert), (grouped, up_weight, down_weight))
    results = results.reshape(experts, block_count, CAP, model_width).transpose(1, 0, 2, 3).reshape(-1, model_width)
    expert_out = results[slot_index].reshape(middle.shape)
    return middle + gate_value * expert_out

def reference(tokens, out_grad, attention_gain, query_weight, key_weight, value_weight, output_weight, position_bias, bucket_table, feedforward_gain, router_matrix, routes, up_weight, down_weight):
    floats = (tokens, attention_gain, query_weight, key_weight, value_weight, output_weight, position_bias, feedforward_gain, router_matrix, up_weight, down_weight)
    floats = tuple((argument.astype(jnp.float32) for argument in floats))

    def forward(*weights):
        return encoder_block_pass(*weights, bucket_table, routes)
    output, pullback = jax.vjp(forward, *floats)
    gradients = pullback(out_grad.astype(jnp.float32))
    return (output.astype(jnp.bfloat16), gradients[0], gradients[1], gradients[2], gradients[3], gradients[4], gradients[5], gradients[6], gradients[7], gradients[8], gradients[9], gradients[10])
```

```python
from functools import partial

import jax
import jax.numpy as jnp
from jax import lax
from jax.experimental import pallas as pl
from jax.experimental.pallas import tpu as pltpu
from jax.sharding import PartitionSpec as P

BUCKETS = 32
EPSILON = 1e-06
TILE = 128
VMEM_BYTES = 48 * 1024 * 1024
BF16 = jnp.bfloat16
F32 = jnp.float32


def dot_nn(left, right):
    return jnp.dot(left, right, preferred_element_type=F32)


def dot_nt(left, right):
    return lax.dot_general(left, right, (((1,), (1,)), ((), ())), preferred_element_type=F32)


def dot_tn(left, right):
    return lax.dot_general(left, right, (((0,), (0,)), ((), ())), preferred_element_type=F32)


def skew_kernel(offset_ref, skewed_ref):
    heads, width = skewed_ref.shape[0], skewed_ref.shape[2]
    row = lax.broadcasted_iota(jnp.int32, (8, width), 0)
    for head in range(heads):
        base = jnp.broadcast_to(offset_ref[head : head + 1, :], (8, width))
        part = pltpu.roll(base, width - (TILE - 1), axis=1)
        for bit in (1, 2, 4):
            part = jnp.where((row & bit) != 0, pltpu.roll(part, bit, axis=1), part)
        for step in (8, 16, 32, 64):
            part = jnp.concatenate([part, pltpu.roll(part, step, axis=1)], axis=0)
        skewed_ref[head] = part


def skew_bias(offset_bias, heads):
    width = offset_bias.shape[1]
    return pl.pallas_call(
        skew_kernel,
        out_shape=jax.ShapeDtypeStruct((heads, TILE, width), F32),
        compiler_params=pltpu.CompilerParams(vmem_limit_bytes=VMEM_BYTES),
    )(offset_bias)


def forward_kernel(
    heads, head_size, row_count, tokens_ref, gain_ref, weight_ref, skewed_ref,
    normed_ref, qkv_ref, probs_ref, context_ref, parts,
):
    block = pl.program_id(0)
    length = tokens_ref.shape[0]
    tiles = length // TILE
    width = heads * head_size

    @pl.when(block == 0)
    def _():
        values = tokens_ref[...].astype(F32)
        scale = lax.rsqrt(jnp.mean(values * values, axis=-1, keepdims=True) + EPSILON)
        normed = (values * scale * gain_ref[...]).astype(BF16)
        normed_ref[...] = normed
        qkv = dot_nn(normed, weight_ref[...]).astype(BF16)
        qkv_ref[...] = qkv
        for part in range(3 * heads):
            parts[part] = qkv[:, part * head_size : (part + 1) * head_size]

    first = pl.multiple_of(block * row_count, row_count)
    contexts = []
    for head in range(heads):
        query = parts[head, pl.ds(first, row_count), :]
        scores = dot_nt(query, parts[heads + head])
        biases = []
        for piece in range(row_count // TILE):
            at = (tiles - 1 - piece - block * (row_count // TILE)) * TILE
            biases.append(skewed_ref[head, :, pl.ds(pl.multiple_of(at, TILE), length)])
        scores = scores + jnp.concatenate(biases, axis=0)
        peak = jnp.max(scores, axis=-1, keepdims=True)
        raised = jnp.exp(scores - peak)
        total = jnp.sum(raised, axis=-1, keepdims=True)
        probs = (raised * (1.0 / total)).astype(BF16)
        probs_ref[head] = probs
        contexts.append(dot_nn(probs, parts[2 * heads + head]))
    context_ref[...] = jnp.concatenate(contexts, axis=1).astype(BF16)


def attention_forward(tokens, gain, weight, skewed, heads, head_size):
    length, model_width = tokens.shape
    rows = 256
    width = heads * head_size
    return pl.pallas_call(
        partial(forward_kernel, heads, head_size, rows),
        grid=(length // rows,),
        in_specs=[
            pl.BlockSpec((length, model_width), lambda i: (0, 0)),
            pl.BlockSpec((1, model_width), lambda i: (0, 0)),
            pl.BlockSpec((model_width, 3 * width), lambda i: (0, 0)),
            pl.BlockSpec(skewed.shape, lambda i: (0, 0, 0)),
        ],
        out_specs=[
            pl.BlockSpec((length, model_width), lambda i: (0, 0)),
            pl.BlockSpec((length, 3 * width), lambda i: (0, 0)),
            pl.BlockSpec((heads, rows, length), lambda i: (0, i, 0)),
            pl.BlockSpec((rows, width), lambda i: (i, 0)),
        ],
        out_shape=[
            jax.ShapeDtypeStruct((length, model_width), BF16),
            jax.ShapeDtypeStruct((length, 3 * width), BF16),
            jax.ShapeDtypeStruct((heads, length, length), BF16),
            jax.ShapeDtypeStruct((length, width), BF16),
        ],
        scratch_shapes=[pltpu.VMEM((3 * heads, length, head_size), BF16)],
        compiler_params=pltpu.CompilerParams(vmem_limit_bytes=VMEM_BYTES),
        cost_estimate=pl.CostEstimate(
            flops=2 * length * model_width * 3 * width + 4 * length * length * width,
            bytes_accessed=16 * 1024 * 1024,
            transcendentals=heads * length * length,
        ),
    )(tokens, gain, weight, skewed)


def backward_kernel(
    heads, head_size, row_count, qkv_ref, probs_ref, grad_ref,
    dqkv_ref, offset_ref, parts, dkeys, dvalues, diagonals,
):
    block = pl.program_id(0)
    length = qkv_ref.shape[0]
    tiles = length // TILE
    width = heads * head_size
    span = diagonals.shape[2]

    @pl.when(block == 0)
    def _():
        qkv = qkv_ref[...]
        for part in range(3 * heads):
            parts[part] = qkv[:, part * head_size : (part + 1) * head_size]
        dkeys[...] = jnp.zeros_like(dkeys)
        dvalues[...] = jnp.zeros_like(dvalues)
        diagonals[...] = jnp.zeros_like(diagonals)

    first = pl.multiple_of(block * row_count, row_count)
    grads = grad_ref[...]
    dqueries = []
    for head in range(heads):
        query = parts[head, pl.ds(first, row_count), :]
        grad = grads[:, head * head_size : (head + 1) * head_size]
        probs_low = probs_ref[head]
        probs = probs_low.astype(F32)
        dprobs = dot_nt(grad, parts[2 * heads + head])
        delta = jnp.sum(dprobs * probs, axis=-1, keepdims=True)
        dscores = probs * (dprobs - delta)
        for piece in range(row_count // TILE):
            at = (tiles - 1 - piece - block * (row_count // TILE)) * TILE
            window = pl.ds(pl.multiple_of(at, TILE), length)
            diagonals[head, :, window] += dscores[piece * TILE : (piece + 1) * TILE]
        dscores_low = dscores.astype(BF16)
        dqueries.append(dot_nn(dscores_low, parts[heads + head]))
        dkeys[head] += dot_tn(query, dscores_low)
        dvalues[head] += dot_tn(grad, probs_low)
    dqkv_ref[pl.ds(first, row_count), 0:width] = jnp.concatenate(dqueries, axis=1).astype(BF16)

    @pl.when(block == pl.num_programs(0) - 1)
    def _():
        sides = jnp.concatenate(
            [dkeys[head] for head in range(heads)] + [dvalues[head] for head in range(heads)],
            axis=0,
        )
        dqkv_ref[:, width:] = sides.T.astype(BF16)
        row = lax.broadcasted_iota(jnp.int32, (8, span), 0)
        offset_ref[...] = jnp.zeros_like(offset_ref)
        for head in range(heads):
            part = diagonals[head]
            for step in (64, 32, 16, 8):
                part = part[:step] + pltpu.roll(part[step:], span - step, axis=1)
            for bit in (1, 2, 4):
                part = jnp.where((row & bit) != 0, pltpu.roll(part, span - bit, axis=1), part)
            part = pltpu.roll(part, TILE - 1, axis=1)
            offset_ref[head : head + 1, :] = jnp.sum(part, axis=0, keepdims=True)


def attention_backward(qkv, probs, grad, heads, head_size):
    length = qkv.shape[0]
    rows = 256
    width = heads * head_size
    padded_heads = -(-heads // 8) * 8
    return pl.pallas_call(
        partial(backward_kernel, heads, head_size, rows),
        grid=(length // rows,),
        in_specs=[
            pl.BlockSpec((length, 3 * width), lambda i: (0, 0)),
            pl.BlockSpec((heads, rows, length), lambda i: (0, i, 0)),
            pl.BlockSpec((rows, width), lambda i: (i, 0)),
        ],
        out_specs=[
            pl.BlockSpec((length, 3 * width), lambda i: (0, 0)),
            pl.BlockSpec((padded_heads, 2 * length), lambda i: (0, 0)),
        ],
        out_shape=[
            jax.ShapeDtypeStruct((length, 3 * width), BF16),
            jax.ShapeDtypeStruct((padded_heads, 2 * length), F32),
        ],
        scratch_shapes=[
            pltpu.VMEM((3 * heads, length, head_size), BF16),
            pltpu.VMEM((heads, head_size, length), F32),
            pltpu.VMEM((heads, head_size, length), F32),
            pltpu.VMEM((heads, TILE, 2 * length), F32),
        ],
        compiler_params=pltpu.CompilerParams(vmem_limit_bytes=VMEM_BYTES),
        cost_estimate=pl.CostEstimate(
            flops=8 * length * length * width,
            bytes_accessed=12 * 1024 * 1024,
            transcendentals=0,
        ),
    )(qkv, probs, grad)


def inverse_rms(values):
    return lax.rsqrt(jnp.mean(values * values, axis=-1, keepdims=True) + EPSILON)


def norm_backward(values, inverse, gain, grad):
    scaled = grad * gain
    return inverse * scaled - values * (
        inverse * inverse * inverse * jnp.mean(scaled * values, axis=-1, keepdims=True)
    )


def gather_rows(rows, axis_name):
    count = lax.axis_size(axis_name)
    place = lax.axis_index(axis_name)
    height = rows.shape[0]
    whole = jnp.zeros((count * height,) + rows.shape[1:], rows.dtype)
    whole = lax.dynamic_update_slice_in_dim(whole, rows, place * height, 0)
    for shift in range(1, count):
        moved = lax.ppermute(rows, axis_name, [(j, (j + shift) % count) for j in range(count)])
        origin = lax.rem(place + count - shift, count)
        whole = lax.dynamic_update_slice_in_dim(whole, moved, origin * height, 0)
    return whole


def exchange(parts, axis_name):
    return lax.all_to_all(parts, axis_name, split_axis=0, concat_axis=0, tiled=True)


def per_device(
    tokens,
    out_grad,
    attention_gain,
    query_weight,
    key_weight,
    value_weight,
    output_weight,
    position_bias,
    bucket_table,
    feedforward_gain,
    router_matrix,
    routes,
    up_weight,
    down_weight,
):
    group = ("seq", "shard")
    seq_count = lax.axis_size("seq")
    shard_count = lax.axis_size("shard")
    rep_count = lax.axis_size("rep")
    seq_place = lax.axis_index("seq")
    owner_count = seq_count * shard_count
    seg_rows = tokens.shape[1]
    model_width = tokens.shape[2]
    length = seg_rows * seq_count
    head_count = position_bias.shape[0] * owner_count // BUCKETS
    head_size = model_width // head_count
    heads = head_count // seq_count
    width = heads * head_size
    experts = router_matrix.shape[1]
    capacity = 2 * seg_rows // experts
    shard_rows = query_weight.shape[0]

    token_rows = tokens[0]
    grad_rows = out_grad[0]

    whole_tokens = gather_rows(token_rows, "seq")

    small = jnp.concatenate(
        [attention_gain, feedforward_gain, position_bias, router_matrix.reshape(-1)]
    )
    small_size = small.shape[0]
    small_rows = -(-small_size // (3 * width))
    small = jnp.pad(small, (0, small_rows * 3 * width - small_size)).reshape(small_rows, 3 * width)
    columns = jnp.stack([query_weight, key_weight, value_weight], axis=1)
    columns = columns.reshape(shard_rows, 3, seq_count, width).transpose(2, 0, 1, 3)
    columns = columns.reshape(seq_count, shard_rows, 3 * width)
    packed = jnp.concatenate(
        [columns, jnp.broadcast_to(small[None], (seq_count,) + small.shape)], axis=1
    )
    packed = exchange(packed, "seq")
    packed = lax.all_gather(packed, "shard", axis=1)
    qkv_weight = packed[:, :, :shard_rows].reshape(model_width, 3 * width)
    small_all = packed[:, :, shard_rows:].reshape(owner_count, -1)
    at = 0
    pieces = []
    for size in (shard_rows, shard_rows, position_bias.shape[0], router_matrix.size):
        pieces.append(small_all[:, at : at + size].reshape(-1))
        at += size
    gain_a = pieces[0].astype(F32)[None]
    gain_f = pieces[1].astype(F32)[None]
    bias_table = pieces[2].reshape(BUCKETS, head_count)
    full_router = pieces[3].reshape(model_width, experts)

    chosen = routes[0, :, 0]
    route_marks = (chosen[:, None] == jnp.arange(experts, dtype=jnp.int32)[None, :]).astype(
        jnp.int32
    )
    slot_ranks = jnp.sum((jnp.cumsum(route_marks, axis=0) - route_marks) * route_marks, axis=-1)
    slot_index = chosen * capacity + slot_ranks
    slots = experts * capacity
    place_marks = (
        slot_index[None, :] == jnp.arange(slots, dtype=jnp.int32)[:, None]
    ).astype(BF16)

    def dispatch(rows):
        placed = dot_nn(place_marks, rows).astype(BF16)
        arrived = exchange(placed.reshape(experts, capacity, model_width), group)
        return arrived.reshape(slots, model_width)

    def collect(rows):
        back = exchange(rows.reshape(experts, capacity, model_width), group)
        return dot_tn(place_marks, back.reshape(slots, model_width))

    expert_grads = dispatch(grad_rows)

    output_all = exchange(
        jnp.broadcast_to(output_weight[None], (seq_count,) + output_weight.shape), "seq"
    )
    output_all = lax.all_gather(output_all, "shard", axis=1).reshape(model_width, model_width)
    up_full = lax.all_gather(up_weight, "rep", axis=1, tiled=True)[0]
    down_full = lax.all_gather(down_weight, "rep", axis=1, tiled=True)[0]

    bucket_marks = (
        jnp.pad(bucket_table, (0, 1), constant_values=-1)[None, :]
        == jnp.arange(BUCKETS, dtype=jnp.int32)[:, None]
    ).astype(BF16)
    own_table = lax.dynamic_slice_in_dim(bias_table, seq_place * heads, heads, 1)
    padded_heads = -(-heads // 8) * 8
    own_table = jnp.pad(own_table, ((0, 0), (0, padded_heads - heads)))
    skewed = skew_bias(dot_tn(own_table, bucket_marks), heads)

    normed_whole, qkv, probs, context_own = attention_forward(
        whole_tokens, gain_a, qkv_weight, skewed, heads, head_size
    )
    context = exchange(context_own.reshape(seq_count, seg_rows, width), "seq")
    context = context.transpose(1, 0, 2).reshape(seg_rows, model_width)
    inputs = token_rows.astype(F32)
    grads_out = grad_rows.astype(F32)
    middle = inputs + dot_nn(context, output_all)
    middle_inverse = inverse_rms(middle)
    normed_ffn = (middle * middle_inverse * gain_f).astype(BF16)

    expert_rows = dispatch(normed_ffn)
    owner = seq_place * shard_count + lax.axis_index("shard")
    logits = dot_nn(expert_rows, full_router)
    logit_exp = jnp.exp(logits - jnp.max(logits, axis=-1, keepdims=True))
    router_probs = logit_exp / jnp.sum(logit_exp, axis=-1, keepdims=True)
    picked = (jnp.arange(experts, dtype=jnp.int32) == owner).astype(F32)[None]
    gate = jnp.sum(router_probs * picked, axis=-1, keepdims=True)

    pre_activation = dot_nt(expert_rows, up_full)
    hidden, gelu_back = jax.vjp(jax.nn.gelu, pre_activation)
    hidden_low = hidden.astype(BF16)
    expert_out = dot_nn(hidden_low, down_full).astype(BF16).astype(F32)
    expert_grads_wide = expert_grads.astype(F32)
    out_rows_grad = (gate * expert_grads_wide).astype(BF16)
    gate_grad = jnp.sum(expert_grads_wide * expert_out, axis=-1, keepdims=True)
    logit_grad = (gate_grad * gate * (picked - router_probs)).astype(BF16)
    pre_grad = gelu_back(dot_nt(out_rows_grad, down_full))[0].astype(BF16)
    rows_grad = dot_nn(pre_grad, up_full) + dot_nt(logit_grad, full_router)
    normed_ffn_grad = collect(rows_grad.astype(BF16))
    returned = collect((gate * expert_out).astype(BF16))
    layer_output = (middle + returned).astype(BF16)
    router_grad = dot_tn(expert_rows, logit_grad)
    up_grad = dot_tn(pre_grad, expert_rows)
    down_grad = dot_tn(hidden_low, out_rows_grad)
    up_weight_grad = lax.psum_scatter(
        up_grad.astype(BF16)[None], "rep", scatter_dimension=1, tiled=True
    ).astype(F32)
    down_weight_grad = lax.psum_scatter(
        down_grad.astype(BF16)[None], "rep", scatter_dimension=1, tiled=True
    ).astype(F32)

    gain_f_grad = jnp.sum(normed_ffn_grad * middle * middle_inverse, axis=0)
    middle_grad = grads_out + norm_backward(middle, middle_inverse, gain_f, normed_ffn_grad)
    attn_out_grad = middle_grad.astype(BF16)
    context_grad = dot_nt(attn_out_grad, output_all).astype(BF16)
    context_grad = context_grad.reshape(seg_rows, seq_count, width).transpose(1, 0, 2)
    context_grad = exchange(context_grad, "seq").reshape(length, width)
    attn_out_grad_whole = gather_rows(attn_out_grad, "seq")

    dqkv, offset_grad = attention_backward(qkv, probs, context_grad, heads, head_size)
    normed_grad_part = dot_nt(dqkv, qkv_weight)
    qkv_grad = dot_tn(normed_whole, dqkv)
    output_grad = dot_tn(context_own, attn_out_grad_whole)
    wide_tokens = whole_tokens.astype(F32)
    gain_a_grad = jnp.sum(normed_grad_part * wide_tokens * inverse_rms(wide_tokens), axis=0)
    own_table_grad = lax.dot_general(
        bucket_marks.astype(F32),
        offset_grad,
        (((1,), (1,)), ((), ())),
        precision=lax.Precision.HIGHEST,
        preferred_element_type=F32,
    )
    table_grad = lax.dynamic_update_slice_in_dim(
        jnp.zeros((BUCKETS, head_count), F32), own_table_grad[:, :heads], seq_place * heads, 1
    )

    arrived = exchange(
        normed_grad_part.astype(BF16).reshape(seq_count, seg_rows, model_width), "seq"
    )
    normed_grad = jnp.sum(arrived.astype(F32), axis=0)
    token_inverse = inverse_rms(inputs)
    token_input_gradient = middle_grad + norm_backward(inputs, token_inverse, gain_a, normed_grad)

    small_grad = jnp.concatenate(
        [
            gain_a_grad.reshape(owner_count, -1),
            gain_f_grad.reshape(owner_count, -1),
            table_grad.reshape(owner_count, -1),
            router_grad.reshape(owner_count, -1),
        ],
        axis=1,
    )
    small_grad = jnp.pad(small_grad, ((0, 0), (0, small_rows * 3 * width - small_size)))
    weight_parts = jnp.concatenate(
        [
            qkv_grad.reshape(owner_count, shard_rows, 3 * width),
            small_grad.reshape(owner_count, small_rows, 3 * width),
        ],
        axis=1,
    ).astype(BF16)
    weight_parts = exchange(weight_parts, group).astype(F32)
    weight_parts = jnp.sum(
        weight_parts.reshape(seq_count, shard_count, shard_rows + small_rows, 3 * width), axis=1
    )
    small_part = jnp.sum(weight_parts[:, shard_rows:], axis=0).reshape(-1)
    qkv_part = weight_parts[:, :shard_rows].reshape(seq_count, shard_rows, 3, width)
    qkv_part = qkv_part.transpose(2, 1, 0, 3).reshape(-1)
    output_part = exchange(
        output_grad.astype(BF16).reshape(shard_count, shard_rows, model_width), "shard"
    )
    output_part = jnp.sum(output_part.astype(F32), axis=0).reshape(-1)
    flat = jnp.concatenate([qkv_part, output_part, small_part])
    flat_size = flat.shape[0]
    lanes = rep_count * 8 * TILE
    flat = jnp.pad(flat, (0, -flat_size % lanes)).astype(BF16).reshape(rep_count, -1, TILE)
    flat = jnp.sum(exchange(flat, "rep").astype(F32), axis=0).astype(BF16)
    flat = lax.all_gather(flat, "rep", axis=0, tiled=True).reshape(-1).astype(F32)
    square = shard_rows * model_width
    matrices = flat[: 4 * square].reshape(4, shard_rows, model_width)
    smalls = flat[4 * square : 4 * square + small_size]
    table_size = position_bias.shape[0]
    return (
        layer_output[None],
        token_input_gradient[None],
        smalls[:shard_rows],
        matrices[0],
        matrices[1],
        matrices[2],
        matrices[3],
        smalls[2 * shard_rows : 2 * shard_rows + table_size],
        smalls[shard_rows : 2 * shard_rows],
        smalls[2 * shard_rows + table_size :].reshape(shard_rows, experts),
        up_weight_grad,
        down_weight_grad,
    )


def solution(mesh):
    return jax.shard_map(
        per_device,
        mesh=mesh,
        in_specs=(
            P(("rep", "shard"), "seq", None),
            P(("rep", "shard"), "seq", None),
            P(("seq", "shard")),
            P(("seq", "shard"), None),
            P(("seq", "shard"), None),
            P(("seq", "shard"), None),
            P(("seq", "shard"), None),
            P(("seq", "shard")),
            P(),
            P(("seq", "shard")),
            P(("seq", "shard"), None),
            P(("rep", "shard"), "seq", None),
            P(("seq", "shard"), "rep", None),
            P(("seq", "shard"), "rep", None),
        ),
        out_specs=(
            P(("rep", "shard"), "seq", None),
            P(("rep", "shard"), "seq", None),
            P(("seq", "shard")),
            P(("seq", "shard"), None),
            P(("seq", "shard"), None),
            P(("seq", "shard"), None),
            P(("seq", "shard"), None),
            P(("seq", "shard")),
            P(("seq", "shard")),
            P(("seq", "shard"), None),
            P(("seq", "shard"), "rep", None),
            P(("seq", "shard"), "rep", None),
        ),
        check_vma=False,
    )
```

```python
from functools import partial

import jax
import jax.numpy as jnp
from jax import lax
from jax.experimental import pallas as pl
from jax.experimental.pallas import tpu as pltpu
from jax.sharding import PartitionSpec as P

BUCKETS = 32
EPSILON = 1e-06
TILE = 128
VMEM_BYTES = 48 * 1024 * 1024
BF16 = jnp.bfloat16
F32 = jnp.float32


def dot_nn(left, right):
    return jnp.dot(left, right, preferred_element_type=F32)


def dot_nt(left, right):
    return lax.dot_general(left, right, (((1,), (1,)), ((), ())), preferred_element_type=F32)


def dot_tn(left, right):
    return lax.dot_general(left, right, (((0,), (0,)), ((), ())), preferred_element_type=F32)


def skew_kernel(offset_ref, skewed_ref):
    heads, width = skewed_ref.shape[0], skewed_ref.shape[2]
    row = lax.broadcasted_iota(jnp.int32, (8, width), 0)
    for head in range(heads):
        base = jnp.broadcast_to(offset_ref[head : head + 1, :], (8, width))
        part = pltpu.roll(base, width - (TILE - 1), axis=1)
        for bit in (1, 2, 4):
            part = jnp.where((row & bit) != 0, pltpu.roll(part, bit, axis=1), part)
        for step in (8, 16, 32, 64):
            part = jnp.concatenate([part, pltpu.roll(part, step, axis=1)], axis=0)
        skewed_ref[head] = part


def skew_bias(offset_bias, heads):
    width = offset_bias.shape[1]
    return pl.pallas_call(
        skew_kernel,
        out_shape=jax.ShapeDtypeStruct((heads, TILE, width), F32),
        compiler_params=pltpu.CompilerParams(vmem_limit_bytes=VMEM_BYTES),
    )(offset_bias)


def forward_kernel(
    heads, head_size, row_count, tokens_ref, gain_ref, weight_ref, skewed_ref,
    normed_ref, qkv_ref, probs_ref, context_ref, parts,
):
    block = pl.program_id(0)
    length = tokens_ref.shape[0]
    tiles = length // TILE
    width = heads * head_size

    @pl.when(block == 0)
    def _():
        values = tokens_ref[...].astype(F32)
        scale = lax.rsqrt(jnp.mean(values * values, axis=-1, keepdims=True) + EPSILON)
        normed = (values * scale * gain_ref[...]).astype(BF16)
        normed_ref[...] = normed
        for kind in range(3):
            made = dot_nn(normed, weight_ref[kind]).astype(BF16)
            qkv_ref[kind] = made
            for head in range(heads):
                parts[kind * heads + head] = made[:, head * head_size : (head + 1) * head_size]

    first = pl.multiple_of(block * row_count, row_count)
    contexts = []
    for head in range(heads):
        query = parts[head, pl.ds(first, row_count), :]
        scores = dot_nt(query, parts[heads + head])
        biases = []
        for piece in range(row_count // TILE):
            at = (tiles - 1 - piece - block * (row_count // TILE)) * TILE
            biases.append(skewed_ref[head, :, pl.ds(pl.multiple_of(at, TILE), length)])
        scores = scores + jnp.concatenate(biases, axis=0)
        peak = jnp.max(scores, axis=-1, keepdims=True)
        raised = jnp.exp(scores - peak)
        total = jnp.sum(raised, axis=-1, keepdims=True)
        probs = (raised * (1.0 / total)).astype(BF16)
        probs_ref[head] = probs
        contexts.append(dot_nn(probs, parts[2 * heads + head]))
    context_ref[...] = jnp.concatenate(contexts, axis=1).astype(BF16)


def attention_forward(tokens, gain, weight, skewed, heads, head_size):
    length, model_width = tokens.shape
    rows = 256
    width = heads * head_size
    return pl.pallas_call(
        partial(forward_kernel, heads, head_size, rows),
        grid=(length // rows,),
        in_specs=[
            pl.BlockSpec((length, model_width), lambda i: (0, 0)),
            pl.BlockSpec((1, model_width), lambda i: (0, 0)),
            pl.BlockSpec((3, model_width, width), lambda i: (0, 0, 0)),
            pl.BlockSpec(skewed.shape, lambda i: (0, 0, 0)),
        ],
        out_specs=[
            pl.BlockSpec((length, model_width), lambda i: (0, 0)),
            pl.BlockSpec((3, length, width), lambda i: (0, 0, 0)),
            pl.BlockSpec((heads, rows, length), lambda i: (0, i, 0)),
            pl.BlockSpec((rows, width), lambda i: (i, 0)),
        ],
        out_shape=[
            jax.ShapeDtypeStruct((length, model_width), BF16),
            jax.ShapeDtypeStruct((3, length, width), BF16),
            jax.ShapeDtypeStruct((heads, length, length), BF16),
            jax.ShapeDtypeStruct((length, width), BF16),
        ],
        scratch_shapes=[pltpu.VMEM((3 * heads, length, head_size), BF16)],
        compiler_params=pltpu.CompilerParams(vmem_limit_bytes=VMEM_BYTES),
        cost_estimate=pl.CostEstimate(
            flops=2 * length * model_width * 3 * width + 4 * length * length * width,
            bytes_accessed=16 * 1024 * 1024,
            transcendentals=heads * length * length,
        ),
    )(tokens, gain, weight, skewed)


def backward_kernel(
    heads, head_size, row_count, qkv_ref, probs_ref, grad_ref, weight_ref, tokens_ref, normed_ref,
    weight_grad_ref, token_grad_ref, gain_grad_ref, offset_ref,
    parts, dqueries, dkeys, dvalues, diagonals,
):
    block = pl.program_id(0)
    length = qkv_ref.shape[1]
    tiles = length // TILE
    span = diagonals.shape[2]

    @pl.when(block == 0)
    def _():
        for kind in range(3):
            made = qkv_ref[kind]
            for head in range(heads):
                parts[kind * heads + head] = made[:, head * head_size : (head + 1) * head_size]
        dkeys[...] = jnp.zeros_like(dkeys)
        dvalues[...] = jnp.zeros_like(dvalues)
        diagonals[...] = jnp.zeros_like(diagonals)

    first = pl.multiple_of(block * row_count, row_count)
    grads = grad_ref[...]
    made_queries = []
    for head in range(heads):
        query = parts[head, pl.ds(first, row_count), :]
        grad = grads[:, head * head_size : (head + 1) * head_size]
        probs_low = probs_ref[head]
        probs = probs_low.astype(F32)
        dprobs = dot_nt(grad, parts[2 * heads + head])
        delta = jnp.sum(dprobs * probs, axis=-1, keepdims=True)
        dscores = probs * (dprobs - delta)
        for piece in range(row_count // TILE):
            at = (tiles - 1 - piece - block * (row_count // TILE)) * TILE
            window = pl.ds(pl.multiple_of(at, TILE), length)
            diagonals[head, :, window] += dscores[piece * TILE : (piece + 1) * TILE]
        dscores_low = dscores.astype(BF16)
        made_queries.append(dot_nn(dscores_low, parts[heads + head]))
        dkeys[head] += dot_tn(query, dscores_low)
        dvalues[head] += dot_tn(grad, probs_low)
    dqueries[pl.ds(first, row_count), :] = jnp.concatenate(made_queries, axis=1).astype(BF16)

    @pl.when(block == pl.num_programs(0) - 1)
    def _():
        key_side = jnp.concatenate([dkeys[head] for head in range(heads)], axis=0)
        value_side = jnp.concatenate([dvalues[head] for head in range(heads)], axis=0)
        sides = (dqueries[...], key_side.T.astype(BF16), value_side.T.astype(BF16))
        normed = normed_ref[...]
        token_grad = jnp.zeros(tokens_ref.shape, F32)
        for kind in range(3):
            weight_grad_ref[kind] = dot_tn(normed, sides[kind])
            token_grad = token_grad + dot_nt(sides[kind], weight_ref[kind])
        token_grad_ref[...] = token_grad.astype(BF16)
        values = tokens_ref[...].astype(F32)
        scale = lax.rsqrt(jnp.mean(values * values, axis=-1, keepdims=True) + EPSILON)
        gain_grad_ref[...] = jnp.sum(token_grad * values * scale, axis=0, keepdims=True)
        row = lax.broadcasted_iota(jnp.int32, (8, span), 0)
        offset_ref[...] = jnp.zeros_like(offset_ref)
        for head in range(heads):
            part = diagonals[head]
            for step in (64, 32, 16, 8):
                part = part[:step] + pltpu.roll(part[step:], span - step, axis=1)
            for bit in (1, 2, 4):
                part = jnp.where((row & bit) != 0, pltpu.roll(part, span - bit, axis=1), part)
            part = pltpu.roll(part, TILE - 1, axis=1)
            offset_ref[head : head + 1, :] = jnp.sum(part, axis=0, keepdims=True)


def attention_backward(qkv, probs, grad, weight, tokens, normed, heads, head_size):
    length, model_width = tokens.shape
    rows = 256
    width = heads * head_size
    padded_heads = -(-heads // 8) * 8
    return pl.pallas_call(
        partial(backward_kernel, heads, head_size, rows),
        grid=(length // rows,),
        in_specs=[
            pl.BlockSpec((3, length, width), lambda i: (0, 0, 0)),
            pl.BlockSpec((heads, rows, length), lambda i: (0, i, 0)),
            pl.BlockSpec((rows, width), lambda i: (i, 0)),
            pl.BlockSpec((3, model_width, width), lambda i: (0, 0, 0)),
            pl.BlockSpec((length, model_width), lambda i: (0, 0)),
            pl.BlockSpec((length, model_width), lambda i: (0, 0)),
        ],
        out_specs=[
            pl.BlockSpec((3, model_width, width), lambda i: (0, 0, 0)),
            pl.BlockSpec((length, model_width), lambda i: (0, 0)),
            pl.BlockSpec((1, model_width), lambda i: (0, 0)),
            pl.BlockSpec((padded_heads, 2 * length), lambda i: (0, 0)),
        ],
        out_shape=[
            jax.ShapeDtypeStruct((3, model_width, width), F32),
            jax.ShapeDtypeStruct((length, model_width), BF16),
            jax.ShapeDtypeStruct((1, model_width), F32),
            jax.ShapeDtypeStruct((padded_heads, 2 * length), F32),
        ],
        scratch_shapes=[
            pltpu.VMEM((3 * heads, length, head_size), BF16),
            pltpu.VMEM((length, width), BF16),
            pltpu.VMEM((heads, head_size, length), F32),
            pltpu.VMEM((heads, head_size, length), F32),
            pltpu.VMEM((heads, TILE, 2 * length), F32),
        ],
        compiler_params=pltpu.CompilerParams(vmem_limit_bytes=VMEM_BYTES),
        cost_estimate=pl.CostEstimate(
            flops=8 * length * length * width + 12 * length * model_width * width,
            bytes_accessed=16 * 1024 * 1024,
            transcendentals=0,
        ),
    )(qkv, probs, grad, weight, tokens, normed)


def expert_kernel(
    experts, rows_ref, grads_ref, router_ref, picked_ref, up_ref, down_ref,
    up_grad_ref, down_grad_ref, rows_grad_ref, returned_ref, logit_grad_ref,
    out_total, in_total, router_probs, low_grads_ref,
):
    step = pl.program_id(0)
    picked = picked_ref[...]

    @pl.when(step == 0)
    def _():
        logits = dot_nn(rows_ref[...], router_ref[...])
        lane = lax.broadcasted_iota(jnp.int32, logits.shape, 1)
        peak = jnp.max(jnp.where(lane < experts, logits, -jnp.inf), axis=-1, keepdims=True)
        raised = jnp.where(lane < experts, jnp.exp(jnp.minimum(logits - peak, 0.0)), 0.0)
        probs = raised / jnp.sum(raised, axis=-1, keepdims=True)
        router_probs[...] = probs
        gate = jnp.sum(probs * picked, axis=-1, keepdims=True)
        low_grads_ref[...] = (gate * grads_ref[...].astype(F32)).astype(BF16)
        out_total[...] = jnp.zeros_like(out_total)
        in_total[...] = jnp.zeros_like(in_total)

    up = up_ref[...]
    down = down_ref[...]
    pre = dot_nt(rows_ref[...], up)
    hidden_grad = dot_nt(low_grads_ref[...], down)
    slope = 0.7978845608028654
    square = pre * pre
    curve = jnp.tanh(slope * pre * (1.0 + 0.044715 * square))
    half = 0.5 * (1.0 + curve)
    hidden = (pre * half).astype(BF16)
    derivative = half + (0.5 * slope) * pre * (1.0 - curve * curve) * (
        1.0 + (3.0 * 0.044715) * square
    )
    pre_grad = (hidden_grad * derivative).astype(BF16)
    up_grad_ref[...] = dot_tn(pre_grad, rows_ref[...]).astype(BF16)
    down_grad_ref[...] = dot_tn(hidden, low_grads_ref[...]).astype(BF16)
    out_total[...] += dot_nn(hidden, down)
    in_total[...] += dot_nn(pre_grad, up)

    @pl.when(step == pl.num_programs(0) - 1)
    def _():
        probs = router_probs[...]
        gate = jnp.sum(probs * picked, axis=-1, keepdims=True)
        out = out_total[...].astype(BF16).astype(F32)
        gate_grad = jnp.sum(grads_ref[...].astype(F32) * out, axis=-1, keepdims=True)
        logit_grad = (gate_grad * gate * (picked - probs)).astype(BF16)
        logit_grad_ref[...] = logit_grad
        rows_grad_ref[...] = (in_total[...] + dot_nt(logit_grad, router_ref[...])).astype(BF16)
        returned_ref[...] = (gate * out).astype(BF16)


def expert_pass(rows, grads, router, picked, up, down, experts):
    count, model_width = rows.shape
    units = up.shape[0]
    lanes = router.shape[1]
    block = 512
    whole = pl.BlockSpec((count, model_width), lambda i: (0, 0))
    return pl.pallas_call(
        partial(expert_kernel, experts),
        grid=(units // block,),
        in_specs=[
            whole,
            whole,
            pl.BlockSpec((model_width, lanes), lambda i: (0, 0)),
            pl.BlockSpec((1, lanes), lambda i: (0, 0)),
            pl.BlockSpec((block, model_width), lambda i: (i, 0)),
            pl.BlockSpec((block, model_width), lambda i: (i, 0)),
        ],
        out_specs=[
            pl.BlockSpec((block, model_width), lambda i: (i, 0)),
            pl.BlockSpec((block, model_width), lambda i: (i, 0)),
            whole,
            whole,
            pl.BlockSpec((count, lanes), lambda i: (0, 0)),
        ],
        out_shape=[
            jax.ShapeDtypeStruct((units, model_width), BF16),
            jax.ShapeDtypeStruct((units, model_width), BF16),
            jax.ShapeDtypeStruct((count, model_width), BF16),
            jax.ShapeDtypeStruct((count, model_width), BF16),
            jax.ShapeDtypeStruct((count, lanes), BF16),
        ],
        scratch_shapes=[
            pltpu.VMEM((count, model_width), F32),
            pltpu.VMEM((count, model_width), F32),
            pltpu.VMEM((count, lanes), F32),
            pltpu.VMEM((count, model_width), BF16),
        ],
        compiler_params=pltpu.CompilerParams(vmem_limit_bytes=VMEM_BYTES),
        cost_estimate=pl.CostEstimate(
            flops=12 * count * units * model_width,
            bytes_accessed=16 * 1024 * 1024,
            transcendentals=count * units,
        ),
    )(rows, grads, router, picked, up, down)


def inverse_rms(values):
    return lax.rsqrt(jnp.mean(values * values, axis=-1, keepdims=True) + EPSILON)


def norm_backward(values, inverse, gain, grad):
    scaled = grad * gain
    return inverse * scaled - values * (
        inverse * inverse * inverse * jnp.mean(scaled * values, axis=-1, keepdims=True)
    )


def gather_rows(rows, axis_name):
    count = lax.axis_size(axis_name)
    place = lax.axis_index(axis_name)
    height = rows.shape[0]
    whole = jnp.zeros((count * height,) + rows.shape[1:], rows.dtype)
    whole = lax.dynamic_update_slice_in_dim(whole, rows, place * height, 0)
    for shift in range(1, count):
        moved = lax.ppermute(rows, axis_name, [(j, (j + shift) % count) for j in range(count)])
        origin = lax.rem(place + count - shift, count)
        whole = lax.dynamic_update_slice_in_dim(whole, moved, origin * height, 0)
    return whole


def reduce_rows(parts, axis_name):
    count = lax.axis_size(axis_name)
    place = lax.axis_index(axis_name)
    total = lax.dynamic_index_in_dim(parts, place, 0, False).astype(F32)
    for shift in range(1, count):
        target = lax.rem(place + shift, count)
        moved = lax.ppermute(
            lax.dynamic_index_in_dim(parts, target, 0, False).astype(BF16),
            axis_name,
            [(j, (j + shift) % count) for j in range(count)],
        )
        total = total + moved.astype(F32)
    return total


def exchange_by_permutes(piece_for, axis_name):
    count = lax.axis_size(axis_name)
    place = lax.axis_index(axis_name)
    held = [piece_for(place)]
    for shift in range(1, count):
        held.append(
            lax.ppermute(
                piece_for(lax.rem(place + shift, count)),
                axis_name,
                [(j, (j + shift) % count) for j in range(count)],
            )
        )
    return [
        lax.select_n(lax.rem(place + count - origin, count), *held) for origin in range(count)
    ]


def quarters(parts, count):
    lead, rows, lanes = parts.shape
    return parts.reshape(lead, count, rows // count, lanes).transpose(1, 0, 2, 3)


def after(value, *earlier):
    return lax.optimization_barrier((value,) + earlier)[0]


def exchange(parts, axis_name):
    return lax.all_to_all(parts, axis_name, split_axis=0, concat_axis=0, tiled=True)


def per_device(
    tokens,
    out_grad,
    attention_gain,
    query_weight,
    key_weight,
    value_weight,
    output_weight,
    position_bias,
    bucket_table,
    feedforward_gain,
    router_matrix,
    routes,
    up_weight,
    down_weight,
):
    group = ("seq", "shard")
    seq_count = lax.axis_size("seq")
    shard_count = lax.axis_size("shard")
    rep_count = lax.axis_size("rep")
    seq_place = lax.axis_index("seq")
    owner_count = seq_count * shard_count
    seg_rows = tokens.shape[1]
    model_width = tokens.shape[2]
    length = seg_rows * seq_count
    head_count = position_bias.shape[0] * owner_count // BUCKETS
    head_size = model_width // head_count
    heads = head_count // seq_count
    width = heads * head_size
    experts = router_matrix.shape[1]
    capacity = 2 * seg_rows // experts
    shard_rows = query_weight.shape[0]

    token_rows = tokens[0]
    grad_rows = out_grad[0]

    small = jnp.concatenate(
        [attention_gain, feedforward_gain, position_bias, router_matrix.reshape(-1)]
    )
    small_size = small.shape[0]
    small_rows = -(-small_size // (16 * width)) * 16
    small = jnp.pad(small, (0, small_rows * width - small_size)).reshape(small_rows, width)
    stacked = jnp.concatenate([query_weight, key_weight, value_weight], axis=0)

    def weight_piece(target):
        columns = lax.dynamic_slice_in_dim(stacked, target * width, width, 1)
        return jnp.concatenate([columns, small], axis=0)

    packed = jnp.stack(exchange_by_permutes(weight_piece, "seq"))
    whole_tokens = gather_rows(after(token_rows, packed), "seq")
    packed = lax.all_gather(packed, "shard", axis=1)
    qkv_weight = packed[:, :, : 3 * shard_rows].reshape(
        seq_count, shard_count, 3, shard_rows, width
    )
    qkv_weight = qkv_weight.transpose(2, 0, 1, 3, 4).reshape(3, model_width, width)
    small_all = packed[:, :, 3 * shard_rows :].reshape(owner_count, -1)
    at = 0
    pieces = []
    for size in (shard_rows, shard_rows, position_bias.shape[0], router_matrix.size):
        pieces.append(small_all[:, at : at + size].reshape(-1))
        at += size
    gain_a = pieces[0].astype(F32)[None]
    gain_f = pieces[1].astype(F32)[None]
    bias_table = pieces[2].reshape(BUCKETS, head_count)
    full_router = pieces[3].reshape(model_width, experts)

    chosen = routes[0, :, 0]
    route_marks = (chosen[:, None] == jnp.arange(experts, dtype=jnp.int32)[None, :]).astype(
        jnp.int32
    )
    slot_ranks = jnp.sum((jnp.cumsum(route_marks, axis=0) - route_marks) * route_marks, axis=-1)
    slot_index = chosen * capacity + slot_ranks
    slots = experts * capacity
    place_marks = (
        slot_index[None, :] == jnp.arange(slots, dtype=jnp.int32)[:, None]
    ).astype(BF16)

    def dispatch(rows):
        placed = dot_nn(place_marks, rows).astype(BF16)
        arrived = exchange(placed.reshape(experts, capacity, model_width), group)
        return arrived.reshape(slots, model_width)

    def send_back(rows):
        back = exchange(rows.reshape(experts, capacity, model_width), group)
        return back.reshape(slots, model_width)

    output_seq = gather_rows(after(output_weight, whole_tokens), "seq")
    expert_grads = dispatch(after(grad_rows, whole_tokens, qkv_weight))
    up_full = lax.all_gather(up_weight, "rep", axis=1, tiled=True)[0]
    down_full = lax.all_gather(down_weight, "rep", axis=1, tiled=True)[0]

    bucket_marks = (
        jnp.pad(bucket_table, (0, 1), constant_values=-1)[None, :]
        == jnp.arange(BUCKETS, dtype=jnp.int32)[:, None]
    ).astype(BF16)
    own_table = lax.dynamic_slice_in_dim(bias_table, seq_place * heads, heads, 1)
    padded_heads = -(-heads // 8) * 8
    own_table = jnp.pad(own_table, ((0, 0), (0, padded_heads - heads)))
    skewed = skew_bias(dot_tn(own_table, bucket_marks), heads)

    normed_whole, qkv, probs, context_own = attention_forward(
        whole_tokens, gain_a, qkv_weight, skewed, heads, head_size
    )
    output_seq = after(output_seq, context_own)
    output_all = gather_rows(output_seq, "shard").reshape(
        shard_count, seq_count, shard_rows, model_width
    )
    output_all = output_all.transpose(1, 0, 2, 3).reshape(model_width, model_width)
    context_own = after(context_own, expert_grads)
    context = exchange(context_own.reshape(seq_count, seg_rows, width), "seq")
    context = context.transpose(1, 0, 2).reshape(seg_rows, model_width)
    inputs = token_rows.astype(F32)
    grads_out = grad_rows.astype(F32)
    middle = inputs + dot_nn(context, output_all)
    middle_inverse = inverse_rms(middle)
    normed_ffn = (middle * middle_inverse * gain_f).astype(BF16)

    expert_rows = dispatch(normed_ffn)
    owner = seq_place * shard_count + lax.axis_index("shard")
    lanes = -(-experts // TILE) * TILE
    router_lanes = jnp.pad(full_router, ((0, 0), (0, lanes - experts)))
    picked = (jnp.arange(lanes, dtype=jnp.int32) == owner).astype(F32)[None]
    up_grad, down_grad, rows_grad, gated_out, logit_grad = expert_pass(
        expert_rows, expert_grads, router_lanes, picked, up_full, down_full, experts
    )
    grad_back = send_back(rows_grad)
    router_grad = dot_tn(expert_rows, logit_grad)[:, :experts]
    normed_ffn_grad = dot_tn(place_marks, grad_back)
    up_weight_grad = lax.psum_scatter(
        up_grad[None], "rep", scatter_dimension=1, tiled=True
    ).astype(F32)
    down_weight_grad = lax.psum_scatter(
        down_grad[None], "rep", scatter_dimension=1, tiled=True
    ).astype(F32)

    gain_f_grad = jnp.sum(normed_ffn_grad * middle * middle_inverse, axis=0)
    middle_grad = grads_out + norm_backward(middle, middle_inverse, gain_f, normed_ffn_grad)
    attn_out_grad = middle_grad.astype(BF16)
    context_grad = dot_nt(attn_out_grad, output_all).astype(BF16)
    context_grad = context_grad.reshape(seg_rows, seq_count, width).transpose(1, 0, 2)
    context_grad = exchange(context_grad, "seq").reshape(length, width)
    output_grad = dot_tn(context, attn_out_grad).reshape(
        seq_count, shard_count, shard_rows, model_width
    )
    output_grad = reduce_rows(output_grad.transpose(1, 0, 2, 3), "shard")
    output_grad = reduce_rows(quarters(output_grad, rep_count), "rep")
    returned = send_back(after(gated_out, context_grad))

    qkv_grad, normed_grad_part, gain_a_grad, offset_grad = attention_backward(
        qkv, probs, context_grad, qkv_weight, whole_tokens, normed_whole, heads, head_size
    )
    output_part = reduce_rows(output_grad, "seq")
    layer_output = (middle + dot_tn(place_marks, returned)).astype(BF16)
    own_table_grad = lax.dot_general(
        bucket_marks.astype(F32),
        offset_grad,
        (((1,), (1,)), ((), ())),
        precision=lax.Precision.HIGHEST,
        preferred_element_type=F32,
    )
    table_grad = lax.dynamic_update_slice_in_dim(
        jnp.zeros((BUCKETS, head_count), F32), own_table_grad[:, :heads], seq_place * heads, 1
    )

    small_grad = jnp.concatenate(
        [
            gain_a_grad.reshape(owner_count, -1),
            gain_f_grad.reshape(owner_count, -1),
            table_grad.reshape(owner_count, -1),
            router_grad.reshape(owner_count, -1),
        ],
        axis=1,
    )
    small_grad = jnp.pad(small_grad, ((0, 0), (0, small_rows * width - small_size)))
    weight_parts = qkv_grad.reshape(3, seq_count, shard_count, shard_rows, width)
    weight_parts = weight_parts.transpose(2, 1, 0, 3, 4).reshape(
        shard_count, seq_count, 3 * shard_rows, width
    )
    small_grad = small_grad.reshape(seq_count, shard_count, small_rows, width)
    weight_parts = jnp.concatenate([weight_parts, small_grad.transpose(1, 0, 2, 3)], axis=2)
    weight_parts = reduce_rows(weight_parts, "shard")
    weight_parts = reduce_rows(quarters(weight_parts, rep_count), "rep").astype(BF16)
    weight_parts = exchange_by_permutes(
        lambda target: lax.dynamic_index_in_dim(weight_parts, target, 0, False), "seq"
    )
    weight_rows = jnp.concatenate(weight_parts, axis=1)
    normed_grad = reduce_rows(
        normed_grad_part.reshape(seq_count, seg_rows, model_width), "seq"
    )
    token_inverse = inverse_rms(inputs)
    token_input_gradient = middle_grad + norm_backward(inputs, token_inverse, gain_a, normed_grad)

    rows = jnp.concatenate([weight_rows, output_part.astype(BF16)], axis=0)
    rows = gather_rows(rows[None], "rep").astype(F32)
    part_rows = weight_rows.shape[0]
    weight_rows = rows[:, :part_rows].reshape(rep_count * part_rows, model_width)
    output_rows = rows[:, part_rows:].reshape(shard_rows, model_width)
    matrices = [weight_rows[k * shard_rows : (k + 1) * shard_rows] for k in range(3)]
    matrices.append(output_rows)
    smalls = weight_rows[3 * shard_rows :].reshape(small_rows, seq_count, width)
    smalls = jnp.sum(smalls, axis=1).reshape(-1)[:small_size]
    table_size = position_bias.shape[0]
    return (
        layer_output[None],
        token_input_gradient[None],
        smalls[:shard_rows],
        matrices[0],
        matrices[1],
        matrices[2],
        matrices[3],
        smalls[2 * shard_rows : 2 * shard_rows + table_size],
        smalls[shard_rows : 2 * shard_rows],
        smalls[2 * shard_rows + table_size :].reshape(shard_rows, experts),
        up_weight_grad,
        down_weight_grad,
    )


def solution(mesh):
    return jax.shard_map(
        per_device,
        mesh=mesh,
        in_specs=(
            P(("rep", "shard"), "seq", None),
            P(("rep", "shard"), "seq", None),
            P(("seq", "shard")),
            P(("seq", "shard"), None),
            P(("seq", "shard"), None),
            P(("seq", "shard"), None),
            P(("seq", "shard"), None),
            P(("seq", "shard")),
            P(),
            P(("seq", "shard")),
            P(("seq", "shard"), None),
            P(("rep", "shard"), "seq", None),
            P(("seq", "shard"), "rep", None),
            P(("seq", "shard"), "rep", None),
        ),
        out_specs=(
            P(("rep", "shard"), "seq", None),
            P(("rep", "shard"), "seq", None),
            P(("seq", "shard")),
            P(("seq", "shard"), None),
            P(("seq", "shard"), None),
            P(("seq", "shard"), None),
            P(("seq", "shard"), None),
            P(("seq", "shard")),
            P(("seq", "shard")),
            P(("seq", "shard"), None),
            P(("seq", "shard"), "rep", None),
            P(("seq", "shard"), "rep", None),
        ),
        check_vma=False,
    )
```

```python
from functools import partial

import jax
import jax.numpy as jnp
from jax import lax
from jax.experimental import pallas as pl
from jax.experimental.pallas import tpu as pltpu
from jax.sharding import PartitionSpec as P

BUCKETS = 32
EPSILON = 1e-06
TILE = 128
VMEM_BYTES = 48 * 1024 * 1024
BF16 = jnp.bfloat16
F32 = jnp.float32


def dot_nn(left, right):
    return jnp.dot(left, right, preferred_element_type=F32)


def dot_nt(left, right):
    return lax.dot_general(left, right, (((1,), (1,)), ((), ())), preferred_element_type=F32)


def dot_tn(left, right):
    return lax.dot_general(left, right, (((0,), (0,)), ((), ())), preferred_element_type=F32)


def skew_kernel(offset_ref, skewed_ref):
    heads, width = skewed_ref.shape[0], skewed_ref.shape[2]
    row = lax.broadcasted_iota(jnp.int32, (8, width), 0)
    for head in range(heads):
        base = jnp.broadcast_to(offset_ref[head : head + 1, :], (8, width))
        part = pltpu.roll(base, width - (TILE - 1), axis=1)
        for bit in (1, 2, 4):
            part = jnp.where((row & bit) != 0, pltpu.roll(part, bit, axis=1), part)
        for step in (8, 16, 32, 64):
            part = jnp.concatenate([part, pltpu.roll(part, step, axis=1)], axis=0)
        skewed_ref[head] = part


def skew_bias(offset_bias, heads):
    width = offset_bias.shape[1]
    return pl.pallas_call(
        skew_kernel,
        out_shape=jax.ShapeDtypeStruct((heads, TILE, width), F32),
        compiler_params=pltpu.CompilerParams(vmem_limit_bytes=VMEM_BYTES),
    )(offset_bias)


def forward_kernel(
    heads, head_size, row_count, tokens_ref, gain_ref, weight_ref, skewed_ref,
    normed_ref, qkv_ref, probs_ref, context_ref, parts,
):
    block = pl.program_id(0)
    length = tokens_ref.shape[0]
    tiles = length // TILE
    width = heads * head_size

    @pl.when(block == 0)
    def _():
        values = tokens_ref[...].astype(F32)
        scale = lax.rsqrt(jnp.mean(values * values, axis=-1, keepdims=True) + EPSILON)
        normed = (values * scale * gain_ref[...]).astype(BF16)
        normed_ref[...] = normed
        for kind in range(3):
            made = dot_nn(normed, weight_ref[kind]).astype(BF16)
            qkv_ref[kind] = made
            for head in range(heads):
                parts[kind * heads + head] = made[:, head * head_size : (head + 1) * head_size]

    first = pl.multiple_of(block * row_count, row_count)
    contexts = []
    for head in range(heads):
        query = parts[head, pl.ds(first, row_count), :]
        scores = dot_nt(query, parts[heads + head])
        biases = []
        for piece in range(row_count // TILE):
            at = (tiles - 1 - piece - block * (row_count // TILE)) * TILE
            biases.append(skewed_ref[head, :, pl.ds(pl.multiple_of(at, TILE), length)])
        scores = scores + jnp.concatenate(biases, axis=0)
        peak = jnp.max(scores, axis=-1, keepdims=True)
        raised = jnp.exp(scores - peak)
        total = jnp.sum(raised, axis=-1, keepdims=True)
        probs = (raised * (1.0 / total)).astype(BF16)
        probs_ref[head] = probs
        contexts.append(dot_nn(probs, parts[2 * heads + head]))
    context_ref[...] = jnp.concatenate(contexts, axis=1).astype(BF16)


def attention_forward(tokens, gain, weight, skewed, heads, head_size):
    length, model_width = tokens.shape
    rows = 256
    width = heads * head_size
    return pl.pallas_call(
        partial(forward_kernel, heads, head_size, rows),
        grid=(length // rows,),
        in_specs=[
            pl.BlockSpec((length, model_width), lambda i: (0, 0)),
            pl.BlockSpec((1, model_width), lambda i: (0, 0)),
            pl.BlockSpec((3, model_width, width), lambda i: (0, 0, 0)),
            pl.BlockSpec(skewed.shape, lambda i: (0, 0, 0)),
        ],
        out_specs=[
            pl.BlockSpec((length, model_width), lambda i: (0, 0)),
            pl.BlockSpec((3, length, width), lambda i: (0, 0, 0)),
            pl.BlockSpec((heads, rows, length), lambda i: (0, i, 0)),
            pl.BlockSpec((rows, width), lambda i: (i, 0)),
        ],
        out_shape=[
            jax.ShapeDtypeStruct((length, model_width), BF16),
            jax.ShapeDtypeStruct((3, length, width), BF16),
            jax.ShapeDtypeStruct((heads, length, length), BF16),
            jax.ShapeDtypeStruct((length, width), BF16),
        ],
        scratch_shapes=[pltpu.VMEM((3 * heads, length, head_size), BF16)],
        compiler_params=pltpu.CompilerParams(vmem_limit_bytes=VMEM_BYTES),
        cost_estimate=pl.CostEstimate(
            flops=2 * length * model_width * 3 * width + 4 * length * length * width,
            bytes_accessed=16 * 1024 * 1024,
            transcendentals=heads * length * length,
        ),
    )(tokens, gain, weight, skewed)


def backward_kernel(
    heads, head_size, row_count, qkv_ref, probs_ref, grad_ref, weight_ref, tokens_ref, normed_ref,
    context_ref, out_grad_ref, output_grad_ref, weight_grad_ref, token_grad_ref, gain_grad_ref, offset_ref,
    parts, dqueries, dkeys, dvalues, diagonals,
):
    block = pl.program_id(0)
    length = qkv_ref.shape[1]
    tiles = length // TILE
    span = diagonals.shape[2]

    @pl.when(block == 0)
    def _():
        for kind in range(3):
            made = qkv_ref[kind]
            for head in range(heads):
                parts[kind * heads + head] = made[:, head * head_size : (head + 1) * head_size]
        output_grad = dot_tn(context_ref[...], out_grad_ref[...])
        lanes = output_grad_ref.shape[2]
        for part in range(output_grad_ref.shape[0]):
            output_grad_ref[part] = output_grad[:, part * lanes : (part + 1) * lanes]
        dkeys[...] = jnp.zeros_like(dkeys)
        dvalues[...] = jnp.zeros_like(dvalues)
        diagonals[...] = jnp.zeros_like(diagonals)

    first = pl.multiple_of(block * row_count, row_count)
    grads = grad_ref[...]
    made_queries = []
    for head in range(heads):
        query = parts[head, pl.ds(first, row_count), :]
        grad = grads[:, head * head_size : (head + 1) * head_size]
        probs_low = probs_ref[head]
        probs = probs_low.astype(F32)
        dprobs = dot_nt(grad, parts[2 * heads + head])
        delta = jnp.sum(dprobs * probs, axis=-1, keepdims=True)
        dscores = probs * (dprobs - delta)
        for piece in range(row_count // TILE):
            at = (tiles - 1 - piece - block * (row_count // TILE)) * TILE
            window = pl.ds(pl.multiple_of(at, TILE), length)
            diagonals[head, :, window] += dscores[piece * TILE : (piece + 1) * TILE]
        dscores_low = dscores.astype(BF16)
        made_queries.append(dot_nn(dscores_low, parts[heads + head]))
        dkeys[head] += dot_tn(query, dscores_low)
        dvalues[head] += dot_tn(grad, probs_low)
    dqueries[pl.ds(first, row_count), :] = jnp.concatenate(made_queries, axis=1).astype(BF16)

    @pl.when(block == pl.num_programs(0) - 1)
    def _():
        key_side = jnp.concatenate([dkeys[head] for head in range(heads)], axis=0)
        value_side = jnp.concatenate([dvalues[head] for head in range(heads)], axis=0)
        sides = (dqueries[...], key_side.T.astype(BF16), value_side.T.astype(BF16))
        normed = normed_ref[...]
        token_grad = jnp.zeros(tokens_ref.shape, F32)
        for kind in range(3):
            weight_grad_ref[kind] = dot_tn(normed, sides[kind])
            token_grad = token_grad + dot_nt(sides[kind], weight_ref[kind])
        token_grad_ref[...] = token_grad.astype(BF16)
        values = tokens_ref[...].astype(F32)
        scale = lax.rsqrt(jnp.mean(values * values, axis=-1, keepdims=True) + EPSILON)
        gain_grad_ref[...] = jnp.sum(token_grad * values * scale, axis=0, keepdims=True)
        row = lax.broadcasted_iota(jnp.int32, (8, span), 0)
        offset_ref[...] = jnp.zeros_like(offset_ref)
        for head in range(heads):
            part = diagonals[head]
            for step in (64, 32, 16, 8):
                part = part[:step] + pltpu.roll(part[step:], span - step, axis=1)
            for bit in (1, 2, 4):
                part = jnp.where((row & bit) != 0, pltpu.roll(part, span - bit, axis=1), part)
            part = pltpu.roll(part, TILE - 1, axis=1)
            offset_ref[head : head + 1, :] = jnp.sum(part, axis=0, keepdims=True)


def attention_backward(
    qkv, probs, grad, weight, tokens, normed, context, out_grad, heads, head_size, parts
):
    length, model_width = tokens.shape
    rows = 256
    width = heads * head_size
    padded_heads = -(-heads // 8) * 8
    return pl.pallas_call(
        partial(backward_kernel, heads, head_size, rows),
        grid=(length // rows,),
        in_specs=[
            pl.BlockSpec((3, length, width), lambda i: (0, 0, 0)),
            pl.BlockSpec((heads, rows, length), lambda i: (0, i, 0)),
            pl.BlockSpec((rows, width), lambda i: (i, 0)),
            pl.BlockSpec((3, model_width, width), lambda i: (0, 0, 0)),
            pl.BlockSpec((length, model_width), lambda i: (0, 0)),
            pl.BlockSpec((length, model_width), lambda i: (0, 0)),
            pl.BlockSpec(context.shape, lambda i: (0, 0)),
            pl.BlockSpec(context.shape, lambda i: (0, 0)),
        ],
        out_specs=[
            pl.BlockSpec((parts, model_width, model_width // parts), lambda i: (0, 0, 0)),
            pl.BlockSpec((3, model_width, width), lambda i: (0, 0, 0)),
            pl.BlockSpec((length, model_width), lambda i: (0, 0)),
            pl.BlockSpec((1, model_width), lambda i: (0, 0)),
            pl.BlockSpec((padded_heads, 2 * length), lambda i: (0, 0)),
        ],
        out_shape=[
            jax.ShapeDtypeStruct((parts, model_width, model_width // parts), F32),
            jax.ShapeDtypeStruct((3, model_width, width), F32),
            jax.ShapeDtypeStruct((length, model_width), BF16),
            jax.ShapeDtypeStruct((1, model_width), F32),
            jax.ShapeDtypeStruct((padded_heads, 2 * length), F32),
        ],
        scratch_shapes=[
            pltpu.VMEM((3 * heads, length, head_size), BF16),
            pltpu.VMEM((length, width), BF16),
            pltpu.VMEM((heads, head_size, length), F32),
            pltpu.VMEM((heads, head_size, length), F32),
            pltpu.VMEM((heads, TILE, 2 * length), F32),
        ],
        compiler_params=pltpu.CompilerParams(vmem_limit_bytes=VMEM_BYTES),
        cost_estimate=pl.CostEstimate(
            flops=8 * length * length * width + 12 * length * model_width * width,
            bytes_accessed=16 * 1024 * 1024,
            transcendentals=0,
        ),
    )(qkv, probs, grad, weight, tokens, normed, context, out_grad)


def expert_kernel(
    experts, rows_ref, grads_ref, router_ref, picked_ref, up_ref, down_ref,
    up_grad_ref, down_grad_ref, rows_grad_ref, returned_ref, logit_grad_ref,
    out_total, in_total, router_probs, low_grads_ref,
):
    step = pl.program_id(0)
    picked = picked_ref[...]

    @pl.when(step == 0)
    def _():
        logits = dot_nn(rows_ref[...], router_ref[...])
        lane = lax.broadcasted_iota(jnp.int32, logits.shape, 1)
        peak = jnp.max(jnp.where(lane < experts, logits, -jnp.inf), axis=-1, keepdims=True)
        raised = jnp.where(lane < experts, jnp.exp(jnp.minimum(logits - peak, 0.0)), 0.0)
        probs = raised / jnp.sum(raised, axis=-1, keepdims=True)
        router_probs[...] = probs
        gate = jnp.sum(probs * picked, axis=-1, keepdims=True)
        low_grads_ref[...] = (gate * grads_ref[...].astype(F32)).astype(BF16)
        out_total[...] = jnp.zeros_like(out_total)
        in_total[...] = jnp.zeros_like(in_total)

    up = up_ref[...]
    down = down_ref[...]
    pre = dot_nt(rows_ref[...], up)
    hidden_grad = dot_nt(low_grads_ref[...], down)
    slope = 0.7978845608028654
    square = pre * pre
    curve = jnp.tanh(slope * pre * (1.0 + 0.044715 * square))
    half = 0.5 * (1.0 + curve)
    hidden = (pre * half).astype(BF16)
    derivative = half + (0.5 * slope) * pre * (1.0 - curve * curve) * (
        1.0 + (3.0 * 0.044715) * square
    )
    pre_grad = (hidden_grad * derivative).astype(BF16)
    up_grad_ref[...] = dot_tn(pre_grad, rows_ref[...]).astype(BF16)
    down_grad_ref[...] = dot_tn(hidden, low_grads_ref[...]).astype(BF16)
    out_total[...] += dot_nn(hidden, down)
    in_total[...] += dot_nn(pre_grad, up)

    @pl.when(step == pl.num_programs(0) - 1)
    def _():
        probs = router_probs[...]
        gate = jnp.sum(probs * picked, axis=-1, keepdims=True)
        out = out_total[...].astype(BF16).astype(F32)
        gate_grad = jnp.sum(grads_ref[...].astype(F32) * out, axis=-1, keepdims=True)
        logit_grad = (gate_grad * gate * (picked - probs)).astype(BF16)
        logit_grad_ref[...] = logit_grad
        rows_grad_ref[...] = (in_total[...] + dot_nt(logit_grad, router_ref[...])).astype(BF16)
        returned_ref[...] = (gate * out).astype(BF16)


def expert_pass(rows, grads, router, picked, up, down, experts):
    count, model_width = rows.shape
    units = up.shape[0]
    lanes = router.shape[1]
    block = 512
    whole = pl.BlockSpec((count, model_width), lambda i: (0, 0))
    return pl.pallas_call(
        partial(expert_kernel, experts),
        grid=(units // block,),
        in_specs=[
            whole,
            whole,
            pl.BlockSpec((model_width, lanes), lambda i: (0, 0)),
            pl.BlockSpec((1, lanes), lambda i: (0, 0)),
            pl.BlockSpec((block, model_width), lambda i: (i, 0)),
            pl.BlockSpec((block, model_width), lambda i: (i, 0)),
        ],
        out_specs=[
            pl.BlockSpec((block, model_width), lambda i: (i, 0)),
            pl.BlockSpec((block, model_width), lambda i: (i, 0)),
            whole,
            whole,
            pl.BlockSpec((count, lanes), lambda i: (0, 0)),
        ],
        out_shape=[
            jax.ShapeDtypeStruct((units, model_width), BF16),
            jax.ShapeDtypeStruct((units, model_width), BF16),
            jax.ShapeDtypeStruct((count, model_width), BF16),
            jax.ShapeDtypeStruct((count, model_width), BF16),
            jax.ShapeDtypeStruct((count, lanes), BF16),
        ],
        scratch_shapes=[
            pltpu.VMEM((count, model_width), F32),
            pltpu.VMEM((count, model_width), F32),
            pltpu.VMEM((count, lanes), F32),
            pltpu.VMEM((count, model_width), BF16),
        ],
        compiler_params=pltpu.CompilerParams(vmem_limit_bytes=VMEM_BYTES),
        cost_estimate=pl.CostEstimate(
            flops=12 * count * units * model_width,
            bytes_accessed=16 * 1024 * 1024,
            transcendentals=count * units,
        ),
    )(rows, grads, router, picked, up, down)


def inverse_rms(values):
    return lax.rsqrt(jnp.mean(values * values, axis=-1, keepdims=True) + EPSILON)


def norm_backward(values, inverse, gain, grad):
    scaled = grad * gain
    return inverse * scaled - values * (
        inverse * inverse * inverse * jnp.mean(scaled * values, axis=-1, keepdims=True)
    )


def gather_rows(rows, axis_name):
    count = lax.axis_size(axis_name)
    place = lax.axis_index(axis_name)
    height = rows.shape[0]
    whole = jnp.zeros((count * height,) + rows.shape[1:], rows.dtype)
    whole = lax.dynamic_update_slice_in_dim(whole, rows, place * height, 0)
    for shift in range(1, count):
        moved = lax.ppermute(rows, axis_name, [(j, (j + shift) % count) for j in range(count)])
        origin = lax.rem(place + count - shift, count)
        whole = lax.dynamic_update_slice_in_dim(whole, moved, origin * height, 0)
    return whole


def reduce_rows(parts, axis_name):
    count = lax.axis_size(axis_name)
    place = lax.axis_index(axis_name)
    total = lax.dynamic_index_in_dim(parts, place, 0, False).astype(F32)
    for shift in range(1, count):
        target = lax.rem(place + shift, count)
        moved = lax.ppermute(
            lax.dynamic_index_in_dim(parts, target, 0, False).astype(BF16),
            axis_name,
            [(j, (j + shift) % count) for j in range(count)],
        )
        total = total + moved.astype(F32)
    return total


def exchange_by_permutes(piece_for, axis_name):
    count = lax.axis_size(axis_name)
    place = lax.axis_index(axis_name)
    held = [piece_for(place)]
    for shift in range(1, count):
        held.append(
            lax.ppermute(
                piece_for(lax.rem(place + shift, count)),
                axis_name,
                [(j, (j + shift) % count) for j in range(count)],
            )
        )
    return [
        lax.select_n(lax.rem(place + count - origin, count), *held) for origin in range(count)
    ]


def after(value, *earlier):
    return lax.optimization_barrier((value,) + earlier)[0]


def exchange(parts, axis_name):
    return lax.all_to_all(parts, axis_name, split_axis=0, concat_axis=0, tiled=True)


def per_device(
    tokens,
    out_grad,
    attention_gain,
    query_weight,
    key_weight,
    value_weight,
    output_weight,
    position_bias,
    bucket_table,
    feedforward_gain,
    router_matrix,
    routes,
    up_weight,
    down_weight,
):
    group = ("seq", "shard")
    seq_count = lax.axis_size("seq")
    shard_count = lax.axis_size("shard")
    rep_count = lax.axis_size("rep")
    seq_place = lax.axis_index("seq")
    owner_count = seq_count * shard_count
    seg_rows = tokens.shape[1]
    model_width = tokens.shape[2]
    length = seg_rows * seq_count
    head_count = position_bias.shape[0] * owner_count // BUCKETS
    head_size = model_width // head_count
    heads = head_count // seq_count
    width = heads * head_size
    experts = router_matrix.shape[1]
    capacity = 2 * seg_rows // experts
    shard_rows = query_weight.shape[0]

    token_rows = tokens[0]
    grad_rows = out_grad[0]

    small = jnp.concatenate(
        [attention_gain, feedforward_gain, position_bias, router_matrix.reshape(-1)]
    )
    small_size = small.shape[0]
    step_rows = 16 * rep_count
    part_rows = -(-(3 * shard_rows + -(-small_size // width)) // step_rows) * step_rows
    small_rows = part_rows - 3 * shard_rows
    small = jnp.pad(small, (0, small_rows * width - small_size)).reshape(small_rows, width)
    whole_tokens = gather_rows(token_rows, "seq")
    quarter = model_width // rep_count
    slice_rows = part_rows // rep_count
    rep_place = lax.axis_index("rep")
    stacked = jnp.concatenate(
        [query_weight, key_weight, value_weight, jnp.tile(small, (1, seq_count))], axis=0
    )
    stacked = lax.dynamic_slice_in_dim(stacked, rep_place * slice_rows, slice_rows, 0)
    output_columns = lax.dynamic_slice_in_dim(output_weight, rep_place * quarter, quarter, 1)
    output_columns = output_columns.reshape(-1, width)

    stacked = stacked.reshape(slice_rows, seq_count, width).transpose(1, 0, 2)
    output_columns = jnp.broadcast_to(
        output_columns[None], (seq_count,) + output_columns.shape
    )
    seq_packed = exchange(jnp.concatenate([stacked, output_columns], axis=1), "seq")
    rep_packed = exchange(
        jnp.broadcast_to(seq_packed[None], (rep_count,) + seq_packed.shape), "rep"
    )
    packed = jnp.stack(exchange_by_permutes(lambda target: rep_packed, "shard"))
    parts = packed[:, :, :, :slice_rows].transpose(2, 0, 1, 3, 4)
    parts = parts.reshape(seq_count, shard_count, part_rows, width)
    qkv_weight = parts[:, :, : 3 * shard_rows].reshape(
        seq_count, shard_count, 3, shard_rows, width
    )
    qkv_weight = qkv_weight.transpose(2, 0, 1, 3, 4).reshape(3, model_width, width)
    small_all = parts[:, :, 3 * shard_rows :].reshape(owner_count, -1)
    output_all = packed[:, :, :, slice_rows:].reshape(
        shard_count, rep_count, seq_count, shard_rows, quarter
    )
    output_all = output_all.transpose(2, 0, 3, 1, 4).reshape(model_width, model_width)
    at = 0
    pieces = []
    for size in (shard_rows, shard_rows, position_bias.shape[0], router_matrix.size):
        pieces.append(small_all[:, at : at + size].reshape(-1))
        at += size
    gain_a = pieces[0].astype(F32)[None]
    gain_f = pieces[1].astype(F32)[None]
    bias_table = pieces[2].reshape(BUCKETS, head_count)
    full_router = pieces[3].reshape(model_width, experts)

    chosen = routes[0, :, 0]
    route_marks = (chosen[:, None] == jnp.arange(experts, dtype=jnp.int32)[None, :]).astype(
        jnp.int32
    )
    slot_ranks = jnp.sum((jnp.cumsum(route_marks, axis=0) - route_marks) * route_marks, axis=-1)
    slot_index = chosen * capacity + slot_ranks
    slots = experts * capacity
    place_marks = (
        slot_index[None, :] == jnp.arange(slots, dtype=jnp.int32)[:, None]
    ).astype(BF16)

    def place_rows(rows):
        return dot_nn(place_marks, rows).astype(BF16)

    def dispatch(placed):
        arrived = exchange(placed.reshape(experts, capacity, model_width), group)
        return arrived.reshape(slots, model_width)

    def send_back(rows):
        back = exchange(rows.reshape(experts, capacity, model_width), group)
        return back.reshape(slots, model_width)

    up_full = lax.all_gather(up_weight, "rep", axis=1, tiled=True)[0]
    down_full = lax.all_gather(down_weight, "rep", axis=1, tiled=True)[0]

    bucket_marks = (
        jnp.pad(bucket_table, (0, 1), constant_values=-1)[None, :]
        == jnp.arange(BUCKETS, dtype=jnp.int32)[:, None]
    ).astype(BF16)
    own_table = lax.dynamic_slice_in_dim(bias_table, seq_place * heads, heads, 1)
    padded_heads = -(-heads // 8) * 8
    own_table = jnp.pad(own_table, ((0, 0), (0, padded_heads - heads)))
    skewed = skew_bias(dot_tn(own_table, bucket_marks), heads)

    placed_grads = place_rows(grad_rows)
    whole_tokens, skewed, qkv_weight, placed_grads = lax.optimization_barrier(
        (whole_tokens, skewed, qkv_weight, placed_grads)
    )
    expert_grads = dispatch(placed_grads)

    normed_whole, qkv, probs, context_own = attention_forward(
        whole_tokens, gain_a, qkv_weight, skewed, heads, head_size
    )
    context_own = after(context_own, expert_grads)
    context = exchange(context_own.reshape(seq_count, seg_rows, width), "seq")
    context = context.transpose(1, 0, 2).reshape(seg_rows, model_width)
    inputs = token_rows.astype(F32)
    grads_out = grad_rows.astype(F32)
    middle = inputs + dot_nn(context, output_all)
    middle_inverse = inverse_rms(middle)
    normed_ffn = (middle * middle_inverse * gain_f).astype(BF16)

    expert_rows = dispatch(place_rows(normed_ffn))
    owner = seq_place * shard_count + lax.axis_index("shard")
    lanes = -(-experts // TILE) * TILE
    router_lanes = jnp.pad(full_router, ((0, 0), (0, lanes - experts)))
    picked = (jnp.arange(lanes, dtype=jnp.int32) == owner).astype(F32)[None]
    up_grad, down_grad, rows_grad, gated_out, logit_grad = expert_pass(
        expert_rows, expert_grads, router_lanes, picked, up_full, down_full, experts
    )
    grad_back = send_back(rows_grad)
    router_grad = dot_tn(expert_rows, logit_grad)[:, :experts]
    normed_ffn_grad = dot_tn(place_marks, grad_back)
    up_weight_grad = lax.psum_scatter(
        up_grad[None], "rep", scatter_dimension=1, tiled=True
    ).astype(F32)
    down_weight_grad = lax.psum_scatter(
        down_grad[None], "rep", scatter_dimension=1, tiled=True
    ).astype(F32)

    gain_f_grad = jnp.sum(normed_ffn_grad * middle * middle_inverse, axis=0)
    middle_grad = grads_out + norm_backward(middle, middle_inverse, gain_f, normed_ffn_grad)
    attn_out_grad = middle_grad.astype(BF16)
    context_grad = dot_nt(attn_out_grad, output_all).astype(BF16)
    context_grad = context_grad.reshape(seg_rows, seq_count, width).transpose(1, 0, 2)
    context_grad = exchange(context_grad, "seq").reshape(length, width)
    returned = send_back(after(gated_out, context_grad))

    output_grad, qkv_grad, normed_grad_part, gain_a_grad, offset_grad = attention_backward(
        qkv, probs, context_grad, qkv_weight, whole_tokens, normed_whole,
        context, attn_out_grad, heads, head_size, rep_count,
    )
    output_grad = output_grad.reshape(rep_count, seq_count, shard_count, shard_rows, quarter)
    output_grad = output_grad.transpose(2, 0, 1, 3, 4)
    output_grad = output_grad.reshape(shard_count, rep_count, seq_count, -1, width)
    normed_grad_part = after(normed_grad_part, returned)
    qkv_grad = after(qkv_grad, returned)
    layer_output = (middle + dot_tn(place_marks, returned)).astype(BF16)
    own_table_grad = lax.dot_general(
        bucket_marks.astype(F32),
        offset_grad,
        (((1,), (1,)), ((), ())),
        precision=lax.Precision.HIGHEST,
        preferred_element_type=F32,
    )
    table_grad = lax.dynamic_update_slice_in_dim(
        jnp.zeros((BUCKETS, head_count), F32), own_table_grad[:, :heads], seq_place * heads, 1
    )

    normed_grad = reduce_rows(
        normed_grad_part.reshape(seq_count, seg_rows, model_width), "seq"
    )

    small_grad = jnp.concatenate(
        [
            gain_a_grad.reshape(owner_count, -1),
            gain_f_grad.reshape(owner_count, -1),
            table_grad.reshape(owner_count, -1),
            router_grad.reshape(owner_count, -1),
        ],
        axis=1,
    )
    small_grad = jnp.pad(small_grad, ((0, 0), (0, small_rows * width - small_size)))
    weight_parts = qkv_grad.reshape(3, seq_count, shard_count, shard_rows, width)
    weight_parts = weight_parts.transpose(2, 1, 0, 3, 4).reshape(
        shard_count, seq_count, 3 * shard_rows, width
    )
    small_grad = small_grad.reshape(seq_count, shard_count, small_rows, width)
    weight_parts = jnp.concatenate([weight_parts, small_grad.transpose(1, 0, 2, 3)], axis=2)
    weight_parts = weight_parts.reshape(shard_count, seq_count, rep_count, slice_rows, width)
    weight_parts = jnp.concatenate([weight_parts.transpose(0, 2, 1, 3, 4), output_grad], axis=3)
    weight_parts = reduce_rows(reduce_rows(weight_parts, "shard"), "rep").astype(BF16)
    weight_parts, normed_grad, up_weight_grad = lax.optimization_barrier(
        (weight_parts, normed_grad, up_weight_grad)
    )
    weight_parts = exchange_by_permutes(
        lambda target: lax.dynamic_index_in_dim(weight_parts, target, 0, False), "seq"
    )
    token_inverse = inverse_rms(inputs)
    token_input_gradient = middle_grad + norm_backward(inputs, token_inverse, gain_a, normed_grad)

    output_part = sum(part[slice_rows:].astype(F32) for part in weight_parts).astype(BF16)
    slices = jnp.concatenate([part[:slice_rows] for part in weight_parts] + [output_part], axis=0)
    slices = exchange_by_permutes(lambda target: slices, "rep")
    weight_rows = jnp.concatenate(
        [
            jnp.concatenate(
                [
                    part[origin * slice_rows : (origin + 1) * slice_rows]
                    for origin in range(seq_count)
                ],
                axis=1,
            )
            for part in slices
        ],
        axis=0,
    ).astype(F32)
    matrices = [weight_rows[k * shard_rows : (k + 1) * shard_rows] for k in range(3)]
    output_slices = [
        part[seq_count * slice_rows :].reshape(shard_rows, quarter) for part in slices
    ]
    matrices.append(jnp.concatenate(output_slices, axis=1).astype(F32))
    smalls = weight_rows[3 * shard_rows :].reshape(small_rows, seq_count, width)
    smalls = jnp.sum(smalls, axis=1).reshape(-1)[:small_size]
    table_size = position_bias.shape[0]
    return (
        layer_output[None],
        token_input_gradient[None],
        smalls[:shard_rows],
        matrices[0],
        matrices[1],
        matrices[2],
        matrices[3],
        smalls[2 * shard_rows : 2 * shard_rows + table_size],
        smalls[shard_rows : 2 * shard_rows],
        smalls[2 * shard_rows + table_size :].reshape(shard_rows, experts),
        up_weight_grad,
        down_weight_grad,
    )


def solution(mesh):
    return jax.shard_map(
        per_device,
        mesh=mesh,
        in_specs=(
            P(("rep", "shard"), "seq", None),
            P(("rep", "shard"), "seq", None),
            P(("seq", "shard")),
            P(("seq", "shard"), None),
            P(("seq", "shard"), None),
            P(("seq", "shard"), None),
            P(("seq", "shard"), None),
            P(("seq", "shard")),
            P(),
            P(("seq", "shard")),
            P(("seq", "shard"), None),
            P(("rep", "shard"), "seq", None),
            P(("seq", "shard"), "rep", None),
            P(("seq", "shard"), "rep", None),
        ),
        out_specs=(
            P(("rep", "shard"), "seq", None),
            P(("rep", "shard"), "seq", None),
            P(("seq", "shard")),
            P(("seq", "shard"), None),
            P(("seq", "shard"), None),
            P(("seq", "shard"), None),
            P(("seq", "shard"), None),
            P(("seq", "shard")),
            P(("seq", "shard")),
            P(("seq", "shard"), None),
            P(("seq", "shard"), "rep", None),
            P(("seq", "shard"), "rep", None),
        ),
        check_vma=False,
    )
```

```python
from functools import partial

import jax
import jax.numpy as jnp
from jax import lax
from jax.experimental import pallas as pl
from jax.experimental.pallas import tpu as pltpu
from jax.sharding import PartitionSpec as P

BUCKETS = 32
EPSILON = 1e-06
TILE = 128
VMEM_BYTES = 48 * 1024 * 1024
BF16 = jnp.bfloat16
F32 = jnp.float32


def dot_nn(left, right):
    return jnp.dot(left, right, preferred_element_type=F32)


def dot_nt(left, right):
    return lax.dot_general(left, right, (((1,), (1,)), ((), ())), preferred_element_type=F32)


def dot_tn(left, right):
    return lax.dot_general(left, right, (((0,), (0,)), ((), ())), preferred_element_type=F32)


def skew_kernel(offset_ref, skewed_ref):
    heads, width = skewed_ref.shape[0], skewed_ref.shape[2]
    row = lax.broadcasted_iota(jnp.int32, (8, width), 0)
    for head in range(heads):
        base = jnp.broadcast_to(offset_ref[head : head + 1, :], (8, width))
        part = pltpu.roll(base, width - (TILE - 1), axis=1)
        for bit in (1, 2, 4):
            part = jnp.where((row & bit) != 0, pltpu.roll(part, bit, axis=1), part)
        for step in (8, 16, 32, 64):
            part = jnp.concatenate([part, pltpu.roll(part, step, axis=1)], axis=0)
        skewed_ref[head] = part


def skew_bias(offset_bias, heads):
    width = offset_bias.shape[1]
    return pl.pallas_call(
        skew_kernel,
        out_shape=jax.ShapeDtypeStruct((heads, TILE, width), F32),
        compiler_params=pltpu.CompilerParams(vmem_limit_bytes=VMEM_BYTES),
    )(offset_bias)


def forward_kernel(
    heads, head_size, row_count, tokens_ref, gain_ref, weight_ref, skewed_ref,
    normed_ref, qkv_ref, probs_ref, context_ref, parts,
):
    block = pl.program_id(0)
    length = tokens_ref.shape[0]
    tiles = length // TILE
    width = heads * head_size

    @pl.when(block == 0)
    def _():
        values = tokens_ref[...].astype(F32)
        scale = lax.rsqrt(jnp.mean(values * values, axis=-1, keepdims=True) + EPSILON)
        normed = (values * scale * gain_ref[...]).astype(BF16)
        normed_ref[...] = normed
        for kind in range(3):
            made = dot_nn(normed, weight_ref[kind]).astype(BF16)
            qkv_ref[kind] = made
            for head in range(heads):
                parts[kind * heads + head] = made[:, head * head_size : (head + 1) * head_size]

    first = pl.multiple_of(block * row_count, row_count)
    contexts = []
    for head in range(heads):
        query = parts[head, pl.ds(first, row_count), :]
        scores = dot_nt(query, parts[heads + head])
        biases = []
        for piece in range(row_count // TILE):
            at = (tiles - 1 - piece - block * (row_count // TILE)) * TILE
            biases.append(skewed_ref[head, :, pl.ds(pl.multiple_of(at, TILE), length)])
        scores = scores + jnp.concatenate(biases, axis=0)
        peak = jnp.max(scores, axis=-1, keepdims=True)
        raised = jnp.exp(scores - peak)
        total = jnp.sum(raised, axis=-1, keepdims=True)
        probs = (raised * (1.0 / total)).astype(BF16)
        probs_ref[head] = probs
        contexts.append(dot_nn(probs, parts[2 * heads + head]))
    context_ref[...] = jnp.concatenate(contexts, axis=1).astype(BF16)


def attention_forward(tokens, gain, weight, skewed, heads, head_size):
    length, model_width = tokens.shape
    rows = 512
    width = heads * head_size
    return pl.pallas_call(
        partial(forward_kernel, heads, head_size, rows),
        grid=(length // rows,),
        in_specs=[
            pl.BlockSpec((length, model_width), lambda i: (0, 0)),
            pl.BlockSpec((1, model_width), lambda i: (0, 0)),
            pl.BlockSpec((3, model_width, width), lambda i: (0, 0, 0)),
            pl.BlockSpec(skewed.shape, lambda i: (0, 0, 0)),
        ],
        out_specs=[
            pl.BlockSpec((length, model_width), lambda i: (0, 0)),
            pl.BlockSpec((3, length, width), lambda i: (0, 0, 0)),
            pl.BlockSpec((heads, rows, length), lambda i: (0, i, 0)),
            pl.BlockSpec((rows, width), lambda i: (i, 0)),
        ],
        out_shape=[
            jax.ShapeDtypeStruct((length, model_width), BF16),
            jax.ShapeDtypeStruct((3, length, width), BF16),
            jax.ShapeDtypeStruct((heads, length, length), BF16),
            jax.ShapeDtypeStruct((length, width), BF16),
        ],
        scratch_shapes=[pltpu.VMEM((3 * heads, length, head_size), BF16)],
        compiler_params=pltpu.CompilerParams(vmem_limit_bytes=VMEM_BYTES),
        cost_estimate=pl.CostEstimate(
            flops=2 * length * model_width * 3 * width + 4 * length * length * width,
            bytes_accessed=16 * 1024 * 1024,
            transcendentals=heads * length * length,
        ),
    )(tokens, gain, weight, skewed)


def backward_kernel(
    heads, head_size, row_count, qkv_ref, probs_ref, grad_ref, weight_ref, tokens_ref, normed_ref,
    context_ref, out_grad_ref, packed_ref, token_grad_ref, gain_grad_ref, offset_ref,
    parts, dqueries, dkeys, dvalues, diagonals,
):
    block = pl.program_id(0)
    length = qkv_ref.shape[1]
    tiles = length // TILE
    span = diagonals.shape[2]

    @pl.when(block == 0)
    def _():
        for kind in range(3):
            made = qkv_ref[kind]
            for head in range(heads):
                parts[kind * heads + head] = made[:, head * head_size : (head + 1) * head_size]
        shards, reps, seqs, rows, lanes = packed_ref.shape
        shard_rows = normed_ref.shape[1] // (seqs * shards)
        slice_rows = rows - shard_rows
        for rep in range(3 * shard_rows // slice_rows, reps):
            packed_ref[:, rep] = jnp.zeros((shards, seqs, rows, lanes), BF16)
        output_grad = dot_tn(context_ref[...], out_grad_ref[...]).astype(BF16)
        for rep in range(reps):
            columns = output_grad[:, rep * lanes : (rep + 1) * lanes]
            for owner in range(seqs * shards):
                packed_ref[owner % shards, rep, owner // shards, slice_rows:] = columns[
                    owner * shard_rows : (owner + 1) * shard_rows
                ]
        dkeys[...] = jnp.zeros_like(dkeys)
        dvalues[...] = jnp.zeros_like(dvalues)
        diagonals[...] = jnp.zeros_like(diagonals)

    first = pl.multiple_of(block * row_count, row_count)
    grads = grad_ref[...]
    made_queries = []
    for head in range(heads):
        query = parts[head, pl.ds(first, row_count), :]
        grad = grads[:, head * head_size : (head + 1) * head_size]
        probs_low = probs_ref[head]
        probs = probs_low.astype(F32)
        dprobs = dot_nt(grad, parts[2 * heads + head])
        delta = jnp.sum(dprobs * probs, axis=-1, keepdims=True)
        dscores = probs * (dprobs - delta)
        for piece in range(row_count // TILE):
            at = (tiles - 1 - piece - block * (row_count // TILE)) * TILE
            window = pl.ds(pl.multiple_of(at, TILE), length)
            diagonals[head, :, window] += dscores[piece * TILE : (piece + 1) * TILE]
        dscores_low = dscores.astype(BF16)
        made_queries.append(dot_nn(dscores_low, parts[heads + head]))
        dkeys[head] += dot_tn(query, dscores_low)
        dvalues[head] += dot_tn(grad, probs_low)
    dqueries[pl.ds(first, row_count), :] = jnp.concatenate(made_queries, axis=1).astype(BF16)

    @pl.when(block == pl.num_programs(0) - 1)
    def _():
        key_side = jnp.concatenate([dkeys[head] for head in range(heads)], axis=0)
        value_side = jnp.concatenate([dvalues[head] for head in range(heads)], axis=0)
        sides = (dqueries[...], key_side.T.astype(BF16), value_side.T.astype(BF16))
        shards, reps, seqs, rows, lanes = packed_ref.shape
        shard_rows = normed_ref.shape[1] // (seqs * shards)
        slice_rows = rows - shard_rows
        normed = normed_ref[...]
        token_grad = jnp.zeros(tokens_ref.shape, F32)
        for kind in range(3):
            weight_grad = dot_tn(normed, sides[kind]).astype(BF16)
            for owner in range(seqs * shards):
                at = kind * shard_rows
                stop = at + shard_rows
                while at < stop:
                    until = min(stop, (at // slice_rows + 1) * slice_rows)
                    source = owner * shard_rows + at - kind * shard_rows
                    packed_ref[
                        owner % shards,
                        at // slice_rows,
                        owner // shards,
                        at % slice_rows : at % slice_rows + until - at,
                    ] = weight_grad[source : source + until - at]
                    at = until
            token_grad = token_grad + dot_nt(sides[kind], weight_ref[kind])
        token_grad_ref[...] = token_grad.astype(BF16)
        values = tokens_ref[...].astype(F32)
        scale = lax.rsqrt(jnp.mean(values * values, axis=-1, keepdims=True) + EPSILON)
        gain_grad_ref[...] = jnp.sum(token_grad * values * scale, axis=0, keepdims=True)
        row = lax.broadcasted_iota(jnp.int32, (8, span), 0)
        offset_ref[...] = jnp.zeros_like(offset_ref)
        for head in range(heads):
            part = diagonals[head]
            for step in (64, 32, 16, 8):
                part = part[:step] + pltpu.roll(part[step:], span - step, axis=1)
            for bit in (1, 2, 4):
                part = jnp.where((row & bit) != 0, pltpu.roll(part, span - bit, axis=1), part)
            part = pltpu.roll(part, TILE - 1, axis=1)
            offset_ref[head : head + 1, :] = jnp.sum(part, axis=0, keepdims=True)


def attention_backward(
    qkv, probs, grad, weight, tokens, normed, context, out_grad, heads, head_size, packed_shape
):
    length, model_width = tokens.shape
    rows = 512
    width = heads * head_size
    padded_heads = -(-heads // 8) * 8
    return pl.pallas_call(
        partial(backward_kernel, heads, head_size, rows),
        grid=(length // rows,),
        in_specs=[
            pl.BlockSpec((3, length, width), lambda i: (0, 0, 0)),
            pl.BlockSpec((heads, rows, length), lambda i: (0, i, 0)),
            pl.BlockSpec((rows, width), lambda i: (i, 0)),
            pl.BlockSpec((3, model_width, width), lambda i: (0, 0, 0)),
            pl.BlockSpec((length, model_width), lambda i: (0, 0)),
            pl.BlockSpec((length, model_width), lambda i: (0, 0)),
            pl.BlockSpec(context.shape, lambda i: (0, 0)),
            pl.BlockSpec(context.shape, lambda i: (0, 0)),
        ],
        out_specs=[
            pl.BlockSpec(packed_shape, lambda i: (0, 0, 0, 0, 0)),
            pl.BlockSpec((length, model_width), lambda i: (0, 0)),
            pl.BlockSpec((1, model_width), lambda i: (0, 0)),
            pl.BlockSpec((padded_heads, 2 * length), lambda i: (0, 0)),
        ],
        out_shape=[
            jax.ShapeDtypeStruct(packed_shape, BF16),
            jax.ShapeDtypeStruct((length, model_width), BF16),
            jax.ShapeDtypeStruct((1, model_width), F32),
            jax.ShapeDtypeStruct((padded_heads, 2 * length), F32),
        ],
        scratch_shapes=[
            pltpu.VMEM((3 * heads, length, head_size), BF16),
            pltpu.VMEM((length, width), BF16),
            pltpu.VMEM((heads, head_size, length), F32),
            pltpu.VMEM((heads, head_size, length), F32),
            pltpu.VMEM((heads, TILE, 2 * length), F32),
        ],
        compiler_params=pltpu.CompilerParams(vmem_limit_bytes=VMEM_BYTES),
        cost_estimate=pl.CostEstimate(
            flops=8 * length * length * width + 12 * length * model_width * width,
            bytes_accessed=16 * 1024 * 1024,
            transcendentals=0,
        ),
    )(qkv, probs, grad, weight, tokens, normed, context, out_grad)


def expert_kernel(
    experts, rows_ref, grads_ref, router_ref, picked_ref, up_ref, down_ref,
    weights_grad_ref, rows_grad_ref, returned_ref, logit_grad_ref,
    out_total, in_total, router_probs, low_grads_ref,
):
    step = pl.program_id(0)
    picked = picked_ref[...]

    @pl.when(step == 0)
    def _():
        logits = dot_nn(rows_ref[...], router_ref[...])
        lane = lax.broadcasted_iota(jnp.int32, logits.shape, 1)
        peak = jnp.max(jnp.where(lane < experts, logits, -jnp.inf), axis=-1, keepdims=True)
        raised = jnp.where(lane < experts, jnp.exp(jnp.minimum(logits - peak, 0.0)), 0.0)
        probs = raised / jnp.sum(raised, axis=-1, keepdims=True)
        router_probs[...] = probs
        gate = jnp.sum(probs * picked, axis=-1, keepdims=True)
        low_grads_ref[...] = (gate * grads_ref[...].astype(F32)).astype(BF16)
        out_total[...] = jnp.zeros_like(out_total)
        in_total[...] = jnp.zeros_like(in_total)

    up = up_ref[...]
    down = down_ref[...]
    pre = dot_nt(rows_ref[...], up)
    hidden_grad = dot_nt(low_grads_ref[...], down)
    slope = 0.7978845608028654
    square = pre * pre
    curve = jnp.tanh(slope * pre * (1.0 + 0.044715 * square))
    half = 0.5 * (1.0 + curve)
    hidden = (pre * half).astype(BF16)
    derivative = half + (0.5 * slope) * pre * (1.0 - curve * curve) * (
        1.0 + (3.0 * 0.044715) * square
    )
    pre_grad = (hidden_grad * derivative).astype(BF16)
    weights_grad_ref[0] = dot_tn(pre_grad, rows_ref[...]).astype(BF16)
    weights_grad_ref[1] = dot_tn(hidden, low_grads_ref[...]).astype(BF16)
    out_total[...] += dot_nn(hidden, down)
    in_total[...] += dot_nn(pre_grad, up)

    @pl.when(step == pl.num_programs(0) - 1)
    def _():
        probs = router_probs[...]
        gate = jnp.sum(probs * picked, axis=-1, keepdims=True)
        out = out_total[...].astype(BF16).astype(F32)
        gate_grad = jnp.sum(grads_ref[...].astype(F32) * out, axis=-1, keepdims=True)
        logit_grad = (gate_grad * gate * (picked - probs)).astype(BF16)
        logit_grad_ref[...] = logit_grad
        rows_grad_ref[...] = (in_total[...] + dot_nt(logit_grad, router_ref[...])).astype(BF16)
        returned_ref[...] = (gate * out).astype(BF16)


def expert_pass(rows, grads, router, picked, up, down, experts):
    count, model_width = rows.shape
    units = up.shape[0]
    lanes = router.shape[1]
    block = 1024
    whole = pl.BlockSpec((count, model_width), lambda i: (0, 0))
    return pl.pallas_call(
        partial(expert_kernel, experts),
        grid=(units // block,),
        in_specs=[
            whole,
            whole,
            pl.BlockSpec((model_width, lanes), lambda i: (0, 0)),
            pl.BlockSpec((1, lanes), lambda i: (0, 0)),
            pl.BlockSpec((block, model_width), lambda i: (i, 0)),
            pl.BlockSpec((block, model_width), lambda i: (i, 0)),
        ],
        out_specs=[
            pl.BlockSpec((2, block, model_width), lambda i: (0, i, 0)),
            whole,
            whole,
            pl.BlockSpec((count, lanes), lambda i: (0, 0)),
        ],
        out_shape=[
            jax.ShapeDtypeStruct((2, units, model_width), BF16),
            jax.ShapeDtypeStruct((count, model_width), BF16),
            jax.ShapeDtypeStruct((count, model_width), BF16),
            jax.ShapeDtypeStruct((count, lanes), BF16),
        ],
        scratch_shapes=[
            pltpu.VMEM((count, model_width), F32),
            pltpu.VMEM((count, model_width), F32),
            pltpu.VMEM((count, lanes), F32),
            pltpu.VMEM((count, model_width), BF16),
        ],
        compiler_params=pltpu.CompilerParams(vmem_limit_bytes=VMEM_BYTES),
        cost_estimate=pl.CostEstimate(
            flops=12 * count * units * model_width,
            bytes_accessed=16 * 1024 * 1024,
            transcendentals=count * units,
        ),
    )(rows, grads, router, picked, up, down)


def inverse_rms(values):
    return lax.rsqrt(jnp.mean(values * values, axis=-1, keepdims=True) + EPSILON)


def norm_backward(values, inverse, gain, grad):
    scaled = grad * gain
    return inverse * scaled - values * (
        inverse * inverse * inverse * jnp.mean(scaled * values, axis=-1, keepdims=True)
    )


def gather_rows(rows, axis_name):
    count = lax.axis_size(axis_name)
    place = lax.axis_index(axis_name)
    height = rows.shape[0]
    whole = jnp.zeros((count * height,) + rows.shape[1:], rows.dtype)
    whole = lax.dynamic_update_slice_in_dim(whole, rows, place * height, 0)
    for shift in range(1, count):
        moved = lax.ppermute(rows, axis_name, [(j, (j + shift) % count) for j in range(count)])
        origin = lax.rem(place + count - shift, count)
        whole = lax.dynamic_update_slice_in_dim(whole, moved, origin * height, 0)
    return whole


def reduce_rows(parts, axis_name):
    count = lax.axis_size(axis_name)
    place = lax.axis_index(axis_name)
    total = lax.dynamic_index_in_dim(parts, place, 0, False).astype(F32)
    for shift in range(1, count):
        target = lax.rem(place + shift, count)
        moved = lax.ppermute(
            lax.dynamic_index_in_dim(parts, target, 0, False).astype(BF16),
            axis_name,
            [(j, (j + shift) % count) for j in range(count)],
        )
        total = total + moved.astype(F32)
    return total


def exchange_by_permutes(piece_for, axis_name):
    count = lax.axis_size(axis_name)
    place = lax.axis_index(axis_name)
    held = [piece_for(place)]
    for shift in range(1, count):
        held.append(
            lax.ppermute(
                piece_for(lax.rem(place + shift, count)),
                axis_name,
                [(j, (j + shift) % count) for j in range(count)],
            )
        )
    return [
        lax.select_n(lax.rem(place + count - origin, count), *held) for origin in range(count)
    ]


def after(value, *earlier):
    return lax.optimization_barrier((value,) + earlier)[0]


def exchange(parts, axis_name):
    return lax.all_to_all(parts, axis_name, split_axis=0, concat_axis=0, tiled=True)


def per_device(
    tokens,
    out_grad,
    attention_gain,
    query_weight,
    key_weight,
    value_weight,
    output_weight,
    position_bias,
    bucket_table,
    feedforward_gain,
    router_matrix,
    routes,
    up_weight,
    down_weight,
):
    group = ("seq", "shard")
    seq_count = lax.axis_size("seq")
    shard_count = lax.axis_size("shard")
    rep_count = lax.axis_size("rep")
    seq_place = lax.axis_index("seq")
    owner_count = seq_count * shard_count
    seg_rows = tokens.shape[1]
    model_width = tokens.shape[2]
    length = seg_rows * seq_count
    head_count = position_bias.shape[0] * owner_count // BUCKETS
    head_size = model_width // head_count
    heads = head_count // seq_count
    width = heads * head_size
    experts = router_matrix.shape[1]
    capacity = 2 * seg_rows // experts
    shard_rows = query_weight.shape[0]

    token_rows = tokens[0]
    grad_rows = out_grad[0]

    small = jnp.concatenate(
        [attention_gain, feedforward_gain, position_bias, router_matrix.reshape(-1)]
    )
    small_size = small.shape[0]
    step_rows = 16 * rep_count
    part_rows = -(-(3 * shard_rows + -(-small_size // width)) // step_rows) * step_rows
    small_rows = part_rows - 3 * shard_rows
    small = jnp.pad(small, (0, small_rows * width - small_size)).reshape(small_rows, width)
    whole_tokens = gather_rows(token_rows, "seq")
    quarter = model_width // rep_count
    slice_rows = part_rows // rep_count
    rep_place = lax.axis_index("rep")
    stacked = jnp.concatenate(
        [query_weight, key_weight, value_weight, jnp.tile(small, (1, seq_count))], axis=0
    )
    stacked = lax.dynamic_slice_in_dim(stacked, rep_place * slice_rows, slice_rows, 0)
    output_columns = lax.dynamic_slice_in_dim(output_weight, rep_place * quarter, quarter, 1)
    output_columns = output_columns.reshape(-1, width)

    stacked = stacked.reshape(slice_rows, seq_count, width).transpose(1, 0, 2)
    output_columns = jnp.broadcast_to(
        output_columns[None], (seq_count,) + output_columns.shape
    )
    seq_packed = exchange(jnp.concatenate([stacked, output_columns], axis=1), "seq")
    rep_packed = exchange(
        jnp.broadcast_to(seq_packed[None], (rep_count,) + seq_packed.shape), "rep"
    )
    packed = jnp.stack(exchange_by_permutes(lambda target: rep_packed, "shard"))
    parts = packed[:, :, :, :slice_rows].transpose(2, 0, 1, 3, 4)
    parts = parts.reshape(seq_count, shard_count, part_rows, width)
    qkv_weight = parts[:, :, : 3 * shard_rows].reshape(
        seq_count, shard_count, 3, shard_rows, width
    )
    qkv_weight = qkv_weight.transpose(2, 0, 1, 3, 4).reshape(3, model_width, width)
    small_all = parts[:, :, 3 * shard_rows :].reshape(owner_count, -1)
    output_all = packed[:, :, :, slice_rows:].reshape(
        shard_count, rep_count, seq_count, shard_rows, quarter
    )
    output_all = output_all.transpose(2, 0, 3, 1, 4).reshape(model_width, model_width)
    at = 0
    pieces = []
    for size in (shard_rows, shard_rows, position_bias.shape[0], router_matrix.size):
        pieces.append(small_all[:, at : at + size].reshape(-1))
        at += size
    gain_a = pieces[0].astype(F32)[None]
    gain_f = pieces[1].astype(F32)[None]
    bias_table = pieces[2].reshape(BUCKETS, head_count)
    full_router = pieces[3].reshape(model_width, experts)

    chosen = routes[0, :, 0]
    route_marks = (chosen[:, None] == jnp.arange(experts, dtype=jnp.int32)[None, :]).astype(
        jnp.int32
    )
    slot_ranks = jnp.sum((jnp.cumsum(route_marks, axis=0) - route_marks) * route_marks, axis=-1)
    slot_index = chosen * capacity + slot_ranks
    slots = experts * capacity
    place_marks = (
        slot_index[None, :] == jnp.arange(slots, dtype=jnp.int32)[:, None]
    ).astype(BF16)

    def place_rows(rows):
        return dot_nn(place_marks, rows).astype(BF16)

    def dispatch(placed):
        arrived = exchange(placed.reshape(experts, capacity, model_width), group)
        return arrived.reshape(slots, model_width)

    def send_back(rows):
        back = exchange(rows.reshape(experts, capacity, model_width), group)
        return back.reshape(slots, model_width)

    up_full = lax.all_gather(up_weight, "rep", axis=1, tiled=True)[0]
    down_full = lax.all_gather(down_weight, "rep", axis=1, tiled=True)[0]

    bucket_marks = (
        jnp.pad(bucket_table, (0, 1), constant_values=-1)[None, :]
        == jnp.arange(BUCKETS, dtype=jnp.int32)[:, None]
    ).astype(BF16)
    own_table = lax.dynamic_slice_in_dim(bias_table, seq_place * heads, heads, 1)
    padded_heads = -(-heads // 8) * 8
    own_table = jnp.pad(own_table, ((0, 0), (0, padded_heads - heads)))
    skewed = skew_bias(dot_tn(own_table, bucket_marks), heads)

    placed_grads = place_rows(grad_rows)
    whole_tokens, skewed, qkv_weight, placed_grads = lax.optimization_barrier(
        (whole_tokens, skewed, qkv_weight, placed_grads)
    )
    expert_grads = dispatch(placed_grads)

    normed_whole, qkv, probs, context_own = attention_forward(
        whole_tokens, gain_a, qkv_weight, skewed, heads, head_size
    )
    context_own = after(context_own, expert_grads)
    context = exchange(context_own.reshape(seq_count, seg_rows, width), "seq")
    context = context.transpose(1, 0, 2).reshape(seg_rows, model_width)
    inputs = token_rows.astype(F32)
    grads_out = grad_rows.astype(F32)
    middle = inputs + dot_nn(context, output_all)
    middle_inverse = inverse_rms(middle)
    normed_ffn = (middle * middle_inverse * gain_f).astype(BF16)

    expert_rows = dispatch(place_rows(normed_ffn))
    owner = seq_place * shard_count + lax.axis_index("shard")
    lanes = -(-experts // TILE) * TILE
    router_lanes = jnp.pad(full_router, ((0, 0), (0, lanes - experts)))
    picked = (jnp.arange(lanes, dtype=jnp.int32) == owner).astype(F32)[None]
    expert_weights_grad, rows_grad, gated_out, logit_grad = expert_pass(
        expert_rows, expert_grads, router_lanes, picked, up_full, down_full, experts
    )
    grad_back = send_back(rows_grad)
    router_grad = dot_tn(expert_rows, logit_grad)[:, :experts].reshape(owner_count, -1)
    grad_back, router_grad = lax.optimization_barrier((grad_back, router_grad))
    normed_ffn_grad = dot_tn(place_marks, grad_back)
    expert_weights_grad = lax.psum_scatter(
        expert_weights_grad, "rep", scatter_dimension=1, tiled=True
    ).astype(F32)

    gain_f_grad = jnp.sum(normed_ffn_grad * middle * middle_inverse, axis=0)
    middle_grad = grads_out + norm_backward(middle, middle_inverse, gain_f, normed_ffn_grad)
    attn_out_grad = middle_grad.astype(BF16)
    context_grad = dot_nt(attn_out_grad, output_all).astype(BF16)
    context_grad = context_grad.reshape(seg_rows, seq_count, width).transpose(1, 0, 2)
    context_grad = exchange(context_grad, "seq").reshape(length, width)
    returned = send_back(after(gated_out, context_grad))

    packed_shape = (shard_count, rep_count, seq_count, slice_rows + shard_rows, width)
    weight_parts, normed_grad_part, gain_a_grad, offset_grad = attention_backward(
        qkv, probs, context_grad, qkv_weight, whole_tokens, normed_whole,
        context, attn_out_grad, heads, head_size, packed_shape,
    )
    normed_grad_part = after(normed_grad_part, returned)
    weight_parts = after(weight_parts, returned)
    layer_output = (middle + dot_tn(place_marks, returned)).astype(BF16)
    own_table_grad = lax.dot_general(
        bucket_marks.astype(F32),
        offset_grad,
        (((1,), (1,)), ((), ())),
        precision=lax.Precision.HIGHEST,
        preferred_element_type=F32,
    )
    table_grad = lax.dynamic_update_slice_in_dim(
        jnp.zeros((BUCKETS, head_count), F32), own_table_grad[:, :heads], seq_place * heads, 1
    )

    normed_grad = reduce_rows(
        normed_grad_part.reshape(seq_count, seg_rows, model_width), "seq"
    )

    small_grad = jnp.concatenate(
        [
            gain_a_grad.reshape(owner_count, -1),
            gain_f_grad.reshape(owner_count, -1),
            table_grad.reshape(owner_count, -1),
            router_grad,
        ],
        axis=1,
    )
    small_grad = jnp.pad(small_grad, ((0, 0), (0, small_rows * width - small_size)))
    small_grad = small_grad.reshape(seq_count, shard_count, small_rows, width)
    small_grad = small_grad.transpose(1, 0, 2, 3).astype(BF16)[:, None]
    at = 3 * shard_rows
    while at < part_rows:
        until = min(part_rows, (at // slice_rows + 1) * slice_rows)
        weight_parts = lax.dynamic_update_slice(
            weight_parts,
            small_grad[:, :, :, at - 3 * shard_rows : until - 3 * shard_rows],
            (0, at // slice_rows, 0, at % slice_rows, 0),
        )
        at = until
    weight_parts = reduce_rows(weight_parts, "shard").astype(BF16)
    weight_parts = reduce_rows(weight_parts, "rep").astype(BF16)
    weight_parts, normed_grad = lax.optimization_barrier((weight_parts, normed_grad))
    weight_parts = exchange_by_permutes(
        lambda target: lax.dynamic_index_in_dim(weight_parts, target, 0, False), "seq"
    )
    token_inverse = inverse_rms(inputs)
    token_input_gradient = middle_grad + norm_backward(inputs, token_inverse, gain_a, normed_grad)

    output_part = sum(part[slice_rows:].astype(F32) for part in weight_parts).astype(BF16)
    slices = jnp.concatenate([part[:slice_rows] for part in weight_parts] + [output_part], axis=0)
    slices = exchange_by_permutes(lambda target: slices, "rep")
    weight_rows = jnp.concatenate(
        [
            jnp.concatenate(
                [
                    part[origin * slice_rows : (origin + 1) * slice_rows]
                    for origin in range(seq_count)
                ],
                axis=1,
            )
            for part in slices
        ],
        axis=0,
    ).astype(F32)
    matrices = [weight_rows[k * shard_rows : (k + 1) * shard_rows] for k in range(3)]
    output_slices = [
        part[seq_count * slice_rows :].reshape(shard_rows, quarter) for part in slices
    ]
    matrices.append(jnp.concatenate(output_slices, axis=1).astype(F32))
    smalls = weight_rows[3 * shard_rows :].reshape(small_rows, seq_count, width)
    smalls = jnp.sum(smalls, axis=1).reshape(-1)[:small_size]
    table_size = position_bias.shape[0]
    return (
        layer_output[None],
        token_input_gradient[None],
        smalls[:shard_rows],
        matrices[0],
        matrices[1],
        matrices[2],
        matrices[3],
        smalls[2 * shard_rows : 2 * shard_rows + table_size],
        smalls[shard_rows : 2 * shard_rows],
        smalls[2 * shard_rows + table_size :].reshape(shard_rows, experts),
        expert_weights_grad[:1],
        expert_weights_grad[1:],
    )


def solution(mesh):
    return jax.shard_map(
        per_device,
        mesh=mesh,
        in_specs=(
            P(("rep", "shard"), "seq", None),
            P(("rep", "shard"), "seq", None),
            P(("seq", "shard")),
            P(("seq", "shard"), None),
            P(("seq", "shard"), None),
            P(("seq", "shard"), None),
            P(("seq", "shard"), None),
            P(("seq", "shard")),
            P(),
            P(("seq", "shard")),
            P(("seq", "shard"), None),
            P(("rep", "shard"), "seq", None),
            P(("seq", "shard"), "rep", None),
            P(("seq", "shard"), "rep", None),
        ),
        out_specs=(
            P(("rep", "shard"), "seq", None),
            P(("rep", "shard"), "seq", None),
            P(("seq", "shard")),
            P(("seq", "shard"), None),
            P(("seq", "shard"), None),
            P(("seq", "shard"), None),
            P(("seq", "shard"), None),
            P(("seq", "shard")),
            P(("seq", "shard")),
            P(("seq", "shard"), None),
            P(("seq", "shard"), "rep", None),
            P(("seq", "shard"), "rep", None),
        ),
        check_vma=False,
    )
```

```python
from functools import partial

import jax
import jax.numpy as jnp
from jax import lax
from jax.experimental import pallas as pl
from jax.experimental.pallas import tpu as pltpu
from jax.sharding import PartitionSpec as P

BUCKETS = 32
EPSILON = 1e-06
TILE = 128
VMEM_BYTES = 48 * 1024 * 1024
BF16 = jnp.bfloat16
F32 = jnp.float32


def dot_nn(left, right):
    return jnp.dot(left, right, preferred_element_type=F32)


def dot_nt(left, right):
    return lax.dot_general(left, right, (((1,), (1,)), ((), ())), preferred_element_type=F32)


def dot_tn(left, right):
    return lax.dot_general(left, right, (((0,), (0,)), ((), ())), preferred_element_type=F32)


def skew_bias(offset_ref, skewed_ref):
    heads, width = skewed_ref.shape[0], skewed_ref.shape[2]
    row = lax.broadcasted_iota(jnp.int32, (8, width), 0)
    for head in range(heads):
        base = jnp.broadcast_to(offset_ref[head : head + 1, :], (8, width))
        part = pltpu.roll(base, width - (TILE - 1), axis=1)
        for bit in (1, 2, 4):
            part = jnp.where((row & bit) != 0, pltpu.roll(part, bit, axis=1), part)
        for step in (8, 16, 32, 64):
            part = jnp.concatenate([part, pltpu.roll(part, step, axis=1)], axis=0)
        skewed_ref[head] = part


def forward_kernel(
    heads, head_size, row_count, tokens_ref, gain_ref, weight_ref, offset_ref,
    normed_ref, qkv_ref, probs_ref, context_ref, parts, skewed_ref,
):
    block = pl.program_id(0)
    length = tokens_ref.shape[0]
    tiles = length // TILE
    width = heads * head_size

    @pl.when(block == 0)
    def _():
        skew_bias(offset_ref, skewed_ref)
        values = tokens_ref[...].astype(F32)
        scale = lax.rsqrt(jnp.mean(values * values, axis=-1, keepdims=True) + EPSILON)
        normed = (values * scale * gain_ref[...]).astype(BF16)
        normed_ref[...] = normed
        for kind in range(3):
            made = dot_nn(normed, weight_ref[kind]).astype(BF16)
            qkv_ref[kind] = made
            for head in range(heads):
                parts[kind * heads + head] = made[:, head * head_size : (head + 1) * head_size]

    first = pl.multiple_of(block * row_count, row_count)
    contexts = []
    for head in range(heads):
        query = parts[head, pl.ds(first, row_count), :]
        scores = dot_nt(query, parts[heads + head])
        biases = []
        for piece in range(row_count // TILE):
            at = (tiles - 1 - piece - block * (row_count // TILE)) * TILE
            biases.append(skewed_ref[head, :, pl.ds(pl.multiple_of(at, TILE), length)])
        scores = scores + jnp.concatenate(biases, axis=0)
        peak = jnp.max(scores, axis=-1, keepdims=True)
        raised = jnp.exp(scores - peak)
        total = jnp.sum(raised, axis=-1, keepdims=True)
        probs = (raised * (1.0 / total)).astype(BF16)
        probs_ref[head] = probs
        contexts.append(dot_nn(probs, parts[2 * heads + head]))
    context_ref[...] = jnp.concatenate(contexts, axis=1).astype(BF16)


def attention_forward(tokens, gain, weight, offset_bias, heads, head_size):
    length, model_width = tokens.shape
    rows = 512
    width = heads * head_size
    return pl.pallas_call(
        partial(forward_kernel, heads, head_size, rows),
        grid=(length // rows,),
        in_specs=[
            pl.BlockSpec((length, model_width), lambda i: (0, 0)),
            pl.BlockSpec((1, model_width), lambda i: (0, 0)),
            pl.BlockSpec((3, model_width, width), lambda i: (0, 0, 0)),
            pl.BlockSpec(offset_bias.shape, lambda i: (0, 0)),
        ],
        out_specs=[
            pl.BlockSpec((length, model_width), lambda i: (0, 0)),
            pl.BlockSpec((3, length, width), lambda i: (0, 0, 0)),
            pl.BlockSpec((heads, rows, length), lambda i: (0, i, 0)),
            pl.BlockSpec((rows, width), lambda i: (i, 0)),
        ],
        out_shape=[
            jax.ShapeDtypeStruct((length, model_width), BF16),
            jax.ShapeDtypeStruct((3, length, width), BF16),
            jax.ShapeDtypeStruct((heads, length, length), BF16),
            jax.ShapeDtypeStruct((length, width), BF16),
        ],
        scratch_shapes=[
            pltpu.VMEM((3 * heads, length, head_size), BF16),
            pltpu.VMEM((heads, TILE, 2 * length), F32),
        ],
        compiler_params=pltpu.CompilerParams(vmem_limit_bytes=VMEM_BYTES),
        cost_estimate=pl.CostEstimate(
            flops=2 * length * model_width * 3 * width + 4 * length * length * width,
            bytes_accessed=16 * 1024 * 1024,
            transcendentals=heads * length * length,
        ),
    )(tokens, gain, weight, offset_bias)


def backward_kernel(
    heads, head_size, row_count, qkv_ref, probs_ref, grad_ref, weight_ref, tokens_ref, normed_ref,
    context_ref, out_grad_ref, packed_ref, token_grad_ref, gain_grad_ref, offset_ref,
    parts, dqueries, dkeys, dvalues, diagonals,
):
    block = pl.program_id(0)
    length = qkv_ref.shape[1]
    tiles = length // TILE
    span = diagonals.shape[2]

    @pl.when(block == 0)
    def _():
        for kind in range(3):
            made = qkv_ref[kind]
            for head in range(heads):
                parts[kind * heads + head] = made[:, head * head_size : (head + 1) * head_size]
        shards, reps, seqs, rows, lanes = packed_ref.shape
        shard_rows = normed_ref.shape[1] // (seqs * shards)
        slice_rows = rows - shard_rows
        for rep in range(3 * shard_rows // slice_rows, reps):
            packed_ref[:, rep] = jnp.zeros((shards, seqs, rows, lanes), BF16)
        output_grad = dot_tn(context_ref[...], out_grad_ref[...]).astype(BF16)
        for rep in range(reps):
            columns = output_grad[:, rep * lanes : (rep + 1) * lanes]
            for owner in range(seqs * shards):
                packed_ref[owner % shards, rep, owner // shards, slice_rows:] = columns[
                    owner * shard_rows : (owner + 1) * shard_rows
                ]
        dkeys[...] = jnp.zeros_like(dkeys)
        dvalues[...] = jnp.zeros_like(dvalues)
        diagonals[...] = jnp.zeros_like(diagonals)

    first = pl.multiple_of(block * row_count, row_count)
    grads = grad_ref[...]
    made_queries = []
    for head in range(heads):
        query = parts[head, pl.ds(first, row_count), :]
        grad = grads[:, head * head_size : (head + 1) * head_size]
        probs_low = probs_ref[head]
        probs = probs_low.astype(F32)
        dprobs = dot_nt(grad, parts[2 * heads + head])
        delta = jnp.sum(dprobs * probs, axis=-1, keepdims=True)
        dscores = probs * (dprobs - delta)
        for piece in range(row_count // TILE):
            at = (tiles - 1 - piece - block * (row_count // TILE)) * TILE
            window = pl.ds(pl.multiple_of(at, TILE), length)
            diagonals[head, :, window] += dscores[piece * TILE : (piece + 1) * TILE]
        dscores_low = dscores.astype(BF16)
        made_queries.append(dot_nn(dscores_low, parts[heads + head]))
        dkeys[head] += dot_tn(query, dscores_low)
        dvalues[head] += dot_tn(grad, probs_low)
    dqueries[pl.ds(first, row_count), :] = jnp.concatenate(made_queries, axis=1).astype(BF16)

    @pl.when(block == pl.num_programs(0) - 1)
    def _():
        key_side = jnp.concatenate([dkeys[head] for head in range(heads)], axis=0)
        value_side = jnp.concatenate([dvalues[head] for head in range(heads)], axis=0)
        sides = (dqueries[...], key_side.T.astype(BF16), value_side.T.astype(BF16))
        shards, reps, seqs, rows, lanes = packed_ref.shape
        shard_rows = normed_ref.shape[1] // (seqs * shards)
        slice_rows = rows - shard_rows
        normed = normed_ref[...]
        token_grad = jnp.zeros(tokens_ref.shape, F32)
        for kind in range(3):
            weight_grad = dot_tn(normed, sides[kind]).astype(BF16)
            for owner in range(seqs * shards):
                at = kind * shard_rows
                stop = at + shard_rows
                while at < stop:
                    until = min(stop, (at // slice_rows + 1) * slice_rows)
                    source = owner * shard_rows + at - kind * shard_rows
                    packed_ref[
                        owner % shards,
                        at // slice_rows,
                        owner // shards,
                        at % slice_rows : at % slice_rows + until - at,
                    ] = weight_grad[source : source + until - at]
                    at = until
            token_grad = token_grad + dot_nt(sides[kind], weight_ref[kind])
        token_grad_ref[...] = token_grad.astype(BF16)
        values = tokens_ref[...].astype(F32)
        scale = lax.rsqrt(jnp.mean(values * values, axis=-1, keepdims=True) + EPSILON)
        gain_grad_ref[...] = jnp.sum(token_grad * values * scale, axis=0, keepdims=True)
        row = lax.broadcasted_iota(jnp.int32, (8, span), 0)
        offset_ref[...] = jnp.zeros_like(offset_ref)
        for head in range(heads):
            part = diagonals[head]
            for step in (64, 32, 16, 8):
                part = part[:step] + pltpu.roll(part[step:], span - step, axis=1)
            for bit in (1, 2, 4):
                part = jnp.where((row & bit) != 0, pltpu.roll(part, span - bit, axis=1), part)
            part = pltpu.roll(part, TILE - 1, axis=1)
            offset_ref[head : head + 1, :] = jnp.sum(part, axis=0, keepdims=True)


def attention_backward(
    qkv, probs, grad, weight, tokens, normed, context, out_grad, heads, head_size, packed_shape
):
    length, model_width = tokens.shape
    rows = 512
    width = heads * head_size
    padded_heads = -(-heads // 8) * 8
    return pl.pallas_call(
        partial(backward_kernel, heads, head_size, rows),
        grid=(length // rows,),
        in_specs=[
            pl.BlockSpec((3, length, width), lambda i: (0, 0, 0)),
            pl.BlockSpec((heads, rows, length), lambda i: (0, i, 0)),
            pl.BlockSpec((rows, width), lambda i: (i, 0)),
            pl.BlockSpec((3, model_width, width), lambda i: (0, 0, 0)),
            pl.BlockSpec((length, model_width), lambda i: (0, 0)),
            pl.BlockSpec((length, model_width), lambda i: (0, 0)),
            pl.BlockSpec(context.shape, lambda i: (0, 0)),
            pl.BlockSpec(context.shape, lambda i: (0, 0)),
        ],
        out_specs=[
            pl.BlockSpec(packed_shape, lambda i: (0, 0, 0, 0, 0)),
            pl.BlockSpec((length, model_width), lambda i: (0, 0)),
            pl.BlockSpec((1, model_width), lambda i: (0, 0)),
            pl.BlockSpec((padded_heads, 2 * length), lambda i: (0, 0)),
        ],
        out_shape=[
            jax.ShapeDtypeStruct(packed_shape, BF16),
            jax.ShapeDtypeStruct((length, model_width), BF16),
            jax.ShapeDtypeStruct((1, model_width), F32),
            jax.ShapeDtypeStruct((padded_heads, 2 * length), F32),
        ],
        scratch_shapes=[
            pltpu.VMEM((3 * heads, length, head_size), BF16),
            pltpu.VMEM((length, width), BF16),
            pltpu.VMEM((heads, head_size, length), F32),
            pltpu.VMEM((heads, head_size, length), F32),
            pltpu.VMEM((heads, TILE, 2 * length), F32),
        ],
        compiler_params=pltpu.CompilerParams(vmem_limit_bytes=VMEM_BYTES),
        cost_estimate=pl.CostEstimate(
            flops=8 * length * length * width + 12 * length * model_width * width,
            bytes_accessed=16 * 1024 * 1024,
            transcendentals=0,
        ),
    )(qkv, probs, grad, weight, tokens, normed, context, out_grad)


def expert_kernel(
    experts, rows_ref, grads_ref, router_ref, picked_ref, up_ref, down_ref,
    weights_grad_ref, rows_grad_ref, returned_ref, logit_grad_ref,
    out_total, in_total, router_probs, low_grads_ref,
):
    step = pl.program_id(0)
    picked = picked_ref[...]

    @pl.when(step == 0)
    def _():
        logits = dot_nn(rows_ref[...], router_ref[...])
        lane = lax.broadcasted_iota(jnp.int32, logits.shape, 1)
        peak = jnp.max(jnp.where(lane < experts, logits, -jnp.inf), axis=-1, keepdims=True)
        raised = jnp.where(lane < experts, jnp.exp(jnp.minimum(logits - peak, 0.0)), 0.0)
        probs = raised / jnp.sum(raised, axis=-1, keepdims=True)
        router_probs[...] = probs
        gate = jnp.sum(probs * picked, axis=-1, keepdims=True)
        low_grads_ref[...] = (gate * grads_ref[...].astype(F32)).astype(BF16)
        out_total[...] = jnp.zeros_like(out_total)
        in_total[...] = jnp.zeros_like(in_total)

    up = up_ref[...]
    down = down_ref[...]
    pre = dot_nt(rows_ref[...], up)
    hidden_grad = dot_nt(low_grads_ref[...], down)
    slope = 0.7978845608028654
    square = pre * pre
    curve = jnp.tanh(slope * pre * (1.0 + 0.044715 * square))
    half = 0.5 * (1.0 + curve)
    hidden = (pre * half).astype(BF16)
    derivative = half + (0.5 * slope) * pre * (1.0 - curve * curve) * (
        1.0 + (3.0 * 0.044715) * square
    )
    pre_grad = (hidden_grad * derivative).astype(BF16)
    weights_grad_ref[0] = dot_tn(pre_grad, rows_ref[...]).astype(BF16)
    weights_grad_ref[1] = dot_tn(hidden, low_grads_ref[...]).astype(BF16)
    out_total[...] += dot_nn(hidden, down)
    in_total[...] += dot_nn(pre_grad, up)

    @pl.when(step == pl.num_programs(0) - 1)
    def _():
        probs = router_probs[...]
        gate = jnp.sum(probs * picked, axis=-1, keepdims=True)
        out = out_total[...].astype(BF16).astype(F32)
        gate_grad = jnp.sum(grads_ref[...].astype(F32) * out, axis=-1, keepdims=True)
        logit_grad = (gate_grad * gate * (picked - probs)).astype(BF16)
        logit_grad_ref[...] = logit_grad
        rows_grad_ref[...] = (in_total[...] + dot_nt(logit_grad, router_ref[...])).astype(BF16)
        returned_ref[...] = (gate * out).astype(BF16)


def expert_pass(rows, grads, router, picked, up, down, experts):
    count, model_width = rows.shape
    units = up.shape[0]
    lanes = router.shape[1]
    block = 1024
    whole = pl.BlockSpec((count, model_width), lambda i: (0, 0))
    return pl.pallas_call(
        partial(expert_kernel, experts),
        grid=(units // block,),
        in_specs=[
            whole,
            whole,
            pl.BlockSpec((model_width, lanes), lambda i: (0, 0)),
            pl.BlockSpec((1, lanes), lambda i: (0, 0)),
            pl.BlockSpec((block, model_width), lambda i: (i, 0)),
            pl.BlockSpec((block, model_width), lambda i: (i, 0)),
        ],
        out_specs=[
            pl.BlockSpec((2, block, model_width), lambda i: (0, i, 0)),
            whole,
            whole,
            pl.BlockSpec((count, lanes), lambda i: (0, 0)),
        ],
        out_shape=[
            jax.ShapeDtypeStruct((2, units, model_width), BF16),
            jax.ShapeDtypeStruct((count, model_width), BF16),
            jax.ShapeDtypeStruct((count, model_width), BF16),
            jax.ShapeDtypeStruct((count, lanes), BF16),
        ],
        scratch_shapes=[
            pltpu.VMEM((count, model_width), F32),
            pltpu.VMEM((count, model_width), F32),
            pltpu.VMEM((count, lanes), F32),
            pltpu.VMEM((count, model_width), BF16),
        ],
        compiler_params=pltpu.CompilerParams(vmem_limit_bytes=VMEM_BYTES),
        cost_estimate=pl.CostEstimate(
            flops=12 * count * units * model_width,
            bytes_accessed=16 * 1024 * 1024,
            transcendentals=count * units,
        ),
    )(rows, grads, router, picked, up, down)


def inverse_rms(values):
    return lax.rsqrt(jnp.mean(values * values, axis=-1, keepdims=True) + EPSILON)


def norm_backward(values, inverse, gain, grad):
    scaled = grad * gain
    return inverse * scaled - values * (
        inverse * inverse * inverse * jnp.mean(scaled * values, axis=-1, keepdims=True)
    )


def gather_rows(rows, axis_name):
    count = lax.axis_size(axis_name)
    place = lax.axis_index(axis_name)
    height = rows.shape[0]
    whole = jnp.zeros((count * height,) + rows.shape[1:], rows.dtype)
    whole = lax.dynamic_update_slice_in_dim(whole, rows, place * height, 0)
    for shift in range(1, count):
        moved = lax.ppermute(rows, axis_name, [(j, (j + shift) % count) for j in range(count)])
        origin = lax.rem(place + count - shift, count)
        whole = lax.dynamic_update_slice_in_dim(whole, moved, origin * height, 0)
    return whole


def reduce_rows(parts, axis_name):
    count = lax.axis_size(axis_name)
    place = lax.axis_index(axis_name)
    total = lax.dynamic_index_in_dim(parts, place, 0, False).astype(F32)
    for shift in range(1, count):
        target = lax.rem(place + shift, count)
        moved = lax.ppermute(
            lax.dynamic_index_in_dim(parts, target, 0, False).astype(BF16),
            axis_name,
            [(j, (j + shift) % count) for j in range(count)],
        )
        total = total + moved.astype(F32)
    return total


def exchange_by_permutes(piece_for, axis_name):
    count = lax.axis_size(axis_name)
    place = lax.axis_index(axis_name)
    held = [piece_for(place)]
    for shift in range(1, count):
        held.append(
            lax.ppermute(
                piece_for(lax.rem(place + shift, count)),
                axis_name,
                [(j, (j + shift) % count) for j in range(count)],
            )
        )
    return [
        lax.select_n(lax.rem(place + count - origin, count), *held) for origin in range(count)
    ]


def after(value, *earlier):
    return lax.optimization_barrier((value,) + earlier)[0]


def exchange(parts, axis_name):
    return lax.all_to_all(parts, axis_name, split_axis=0, concat_axis=0, tiled=True)


def per_device(
    tokens,
    out_grad,
    attention_gain,
    query_weight,
    key_weight,
    value_weight,
    output_weight,
    position_bias,
    bucket_table,
    feedforward_gain,
    router_matrix,
    routes,
    up_weight,
    down_weight,
):
    group = ("seq", "shard")
    seq_count = lax.axis_size("seq")
    shard_count = lax.axis_size("shard")
    rep_count = lax.axis_size("rep")
    seq_place = lax.axis_index("seq")
    owner_count = seq_count * shard_count
    seg_rows = tokens.shape[1]
    model_width = tokens.shape[2]
    length = seg_rows * seq_count
    head_count = position_bias.shape[0] * owner_count // BUCKETS
    head_size = model_width // head_count
    heads = head_count // seq_count
    width = heads * head_size
    experts = router_matrix.shape[1]
    capacity = 2 * seg_rows // experts
    shard_rows = query_weight.shape[0]

    token_rows = tokens[0]
    grad_rows = out_grad[0]

    small = jnp.concatenate(
        [attention_gain, feedforward_gain, position_bias, router_matrix.reshape(-1)]
    )
    small_size = small.shape[0]
    step_rows = 16 * rep_count
    part_rows = -(-(3 * shard_rows + -(-small_size // width)) // step_rows) * step_rows
    small_rows = part_rows - 3 * shard_rows
    small = jnp.pad(small, (0, small_rows * width - small_size)).reshape(small_rows, width)
    whole_tokens = gather_rows(token_rows, "seq")
    quarter = model_width // rep_count
    slice_rows = part_rows // rep_count
    rep_place = lax.axis_index("rep")
    stacked = jnp.concatenate(
        [query_weight, key_weight, value_weight, jnp.tile(small, (1, seq_count))], axis=0
    )
    stacked = lax.dynamic_slice_in_dim(stacked, rep_place * slice_rows, slice_rows, 0)
    output_columns = lax.dynamic_slice_in_dim(output_weight, rep_place * quarter, quarter, 1)
    output_columns = output_columns.reshape(-1, width)

    stacked = stacked.reshape(slice_rows, seq_count, width).transpose(1, 0, 2)
    output_columns = jnp.broadcast_to(
        output_columns[None], (seq_count,) + output_columns.shape
    )
    seq_packed = exchange(jnp.concatenate([stacked, output_columns], axis=1), "seq")
    rep_packed = exchange(
        jnp.broadcast_to(seq_packed[None], (rep_count,) + seq_packed.shape), "rep"
    )
    packed = jnp.stack(exchange_by_permutes(lambda target: rep_packed, "shard"))
    parts = packed[:, :, :, :slice_rows].transpose(2, 0, 1, 3, 4)
    parts = parts.reshape(seq_count, shard_count, part_rows, width)
    qkv_weight = parts[:, :, : 3 * shard_rows].reshape(
        seq_count, shard_count, 3, shard_rows, width
    )
    qkv_weight = qkv_weight.transpose(2, 0, 1, 3, 4).reshape(3, model_width, width)
    small_all = parts[:, :, 3 * shard_rows :].reshape(owner_count, -1)
    output_all = packed[:, :, :, slice_rows:].reshape(
        shard_count, rep_count, seq_count, shard_rows, quarter
    )
    output_all = output_all.transpose(2, 0, 3, 1, 4).reshape(model_width, model_width)
    at = 0
    pieces = []
    for size in (shard_rows, shard_rows, position_bias.shape[0], router_matrix.size):
        pieces.append(small_all[:, at : at + size].reshape(-1))
        at += size
    gain_a = pieces[0].astype(F32)[None]
    gain_f = pieces[1].astype(F32)[None]
    bias_table = pieces[2].reshape(BUCKETS, head_count)
    full_router = pieces[3].reshape(model_width, experts)

    chosen = routes[0, :, 0]
    route_marks = (chosen[:, None] == jnp.arange(experts, dtype=jnp.int32)[None, :]).astype(
        jnp.int32
    )
    slot_ranks = jnp.sum((jnp.cumsum(route_marks, axis=0) - route_marks) * route_marks, axis=-1)
    slot_index = chosen * capacity + slot_ranks
    slots = experts * capacity
    place_marks = (
        slot_index[None, :] == jnp.arange(slots, dtype=jnp.int32)[:, None]
    ).astype(BF16)

    def place_rows(rows):
        return dot_nn(place_marks, rows).astype(BF16)

    def dispatch(placed):
        arrived = exchange(placed.reshape(experts, capacity, model_width), group)
        return arrived.reshape(slots, model_width)

    def send_back(rows):
        back = exchange(rows.reshape(experts, capacity, model_width), group)
        return back.reshape(slots, model_width)

    up_full = lax.all_gather(up_weight, "rep", axis=1, tiled=True)[0]
    down_full = lax.all_gather(down_weight, "rep", axis=1, tiled=True)[0]

    bucket_marks = (
        jnp.pad(bucket_table, (0, 1), constant_values=-1)[None, :]
        == jnp.arange(BUCKETS, dtype=jnp.int32)[:, None]
    ).astype(BF16)
    own_table = lax.dynamic_slice_in_dim(bias_table, seq_place * heads, heads, 1)
    padded_heads = -(-heads // 8) * 8
    own_table = jnp.pad(own_table, ((0, 0), (0, padded_heads - heads)))
    offset_bias = dot_tn(own_table, bucket_marks)

    placed_grads = place_rows(grad_rows)
    whole_tokens, offset_bias, qkv_weight, placed_grads = lax.optimization_barrier(
        (whole_tokens, offset_bias, qkv_weight, placed_grads)
    )
    expert_grads = dispatch(placed_grads)

    normed_whole, qkv, probs, context_own = attention_forward(
        whole_tokens, gain_a, qkv_weight, offset_bias, heads, head_size
    )
    context_own = after(context_own, expert_grads)
    context = exchange(context_own.reshape(seq_count, seg_rows, width), "seq")
    context = context.transpose(1, 0, 2).reshape(seg_rows, model_width)
    inputs = token_rows.astype(F32)
    grads_out = grad_rows.astype(F32)
    middle = inputs + dot_nn(context, output_all)
    middle_inverse = inverse_rms(middle)
    normed_ffn = (middle * middle_inverse * gain_f).astype(BF16)

    expert_rows = dispatch(place_rows(normed_ffn))
    owner = seq_place * shard_count + lax.axis_index("shard")
    lanes = -(-experts // TILE) * TILE
    router_lanes = jnp.pad(full_router, ((0, 0), (0, lanes - experts)))
    picked = (jnp.arange(lanes, dtype=jnp.int32) == owner).astype(F32)[None]
    expert_weights_grad, rows_grad, gated_out, logit_grad = expert_pass(
        expert_rows, expert_grads, router_lanes, picked, up_full, down_full, experts
    )
    grad_back = send_back(rows_grad)
    router_grad = dot_tn(expert_rows, logit_grad)[:, :experts].reshape(owner_count, -1)
    grad_back, router_grad = lax.optimization_barrier((grad_back, router_grad))
    normed_ffn_grad = dot_tn(place_marks, grad_back)
    expert_weights_grad = lax.psum_scatter(
        expert_weights_grad, "rep", scatter_dimension=1, tiled=True
    ).astype(F32)

    gain_f_grad = jnp.sum(normed_ffn_grad * middle * middle_inverse, axis=0)
    middle_grad = grads_out + norm_backward(middle, middle_inverse, gain_f, normed_ffn_grad)
    attn_out_grad = middle_grad.astype(BF16)
    context_grad = dot_nt(attn_out_grad, output_all).astype(BF16)
    context_grad = context_grad.reshape(seg_rows, seq_count, width).transpose(1, 0, 2)
    context_grad = exchange(context_grad, "seq").reshape(length, width)
    returned = send_back(after(gated_out, context_grad))

    packed_shape = (shard_count, rep_count, seq_count, slice_rows + shard_rows, width)
    weight_parts, normed_grad_part, gain_a_grad, offset_grad = attention_backward(
        qkv, probs, context_grad, qkv_weight, whole_tokens, normed_whole,
        context, attn_out_grad, heads, head_size, packed_shape,
    )
    normed_grad_part = after(normed_grad_part, returned)
    weight_parts = after(weight_parts, returned)
    layer_output = (middle + dot_tn(place_marks, returned)).astype(BF16)
    own_table_grad = lax.dot_general(
        bucket_marks.astype(F32),
        offset_grad,
        (((1,), (1,)), ((), ())),
        precision=lax.Precision.HIGHEST,
        preferred_element_type=F32,
    )
    table_grad = lax.dynamic_update_slice_in_dim(
        jnp.zeros((BUCKETS, head_count), F32), own_table_grad[:, :heads], seq_place * heads, 1
    )

    normed_grad = reduce_rows(
        normed_grad_part.reshape(seq_count, seg_rows, model_width), "seq"
    )

    small_grad = jnp.concatenate(
        [
            gain_a_grad.reshape(owner_count, -1),
            gain_f_grad.reshape(owner_count, -1),
            table_grad.reshape(owner_count, -1),
            router_grad,
        ],
        axis=1,
    )
    small_grad = jnp.pad(small_grad, ((0, 0), (0, small_rows * width - small_size)))
    small_grad = small_grad.reshape(seq_count, shard_count, small_rows, width)
    small_grad = small_grad.transpose(1, 0, 2, 3).astype(BF16)[:, None]
    at = 3 * shard_rows
    while at < part_rows:
        until = min(part_rows, (at // slice_rows + 1) * slice_rows)
        weight_parts = lax.dynamic_update_slice(
            weight_parts,
            small_grad[:, :, :, at - 3 * shard_rows : until - 3 * shard_rows],
            (0, at // slice_rows, 0, at % slice_rows, 0),
        )
        at = until
    weight_parts = reduce_rows(weight_parts, "shard").astype(BF16)
    weight_parts = reduce_rows(weight_parts, "rep").astype(BF16)
    weight_parts, normed_grad = lax.optimization_barrier((weight_parts, normed_grad))
    weight_parts = exchange_by_permutes(
        lambda target: lax.dynamic_index_in_dim(weight_parts, target, 0, False), "seq"
    )
    token_inverse = inverse_rms(inputs)
    token_input_gradient = middle_grad + norm_backward(inputs, token_inverse, gain_a, normed_grad)

    output_part = sum(part[slice_rows:].astype(F32) for part in weight_parts).astype(BF16)
    slices = jnp.concatenate([part[:slice_rows] for part in weight_parts] + [output_part], axis=0)
    slices = exchange_by_permutes(lambda target: slices, "rep")
    weight_rows = jnp.concatenate(
        [
            jnp.concatenate(
                [
                    part[origin * slice_rows : (origin + 1) * slice_rows]
                    for origin in range(seq_count)
                ],
                axis=1,
            )
            for part in slices
        ],
        axis=0,
    ).astype(F32)
    matrices = [weight_rows[k * shard_rows : (k + 1) * shard_rows] for k in range(3)]
    output_slices = [
        part[seq_count * slice_rows :].reshape(shard_rows, quarter) for part in slices
    ]
    matrices.append(jnp.concatenate(output_slices, axis=1).astype(F32))
    smalls = weight_rows[3 * shard_rows :].reshape(small_rows, seq_count, width)
    smalls = jnp.sum(smalls, axis=1).reshape(-1)[:small_size]
    table_size = position_bias.shape[0]
    return (
        layer_output[None],
        token_input_gradient[None],
        smalls[:shard_rows],
        matrices[0],
        matrices[1],
        matrices[2],
        matrices[3],
        smalls[2 * shard_rows : 2 * shard_rows + table_size],
        smalls[shard_rows : 2 * shard_rows],
        smalls[2 * shard_rows + table_size :].reshape(shard_rows, experts),
        expert_weights_grad[:1],
        expert_weights_grad[1:],
    )


def solution(mesh):
    return jax.shard_map(
        per_device,
        mesh=mesh,
        in_specs=(
            P(("rep", "shard"), "seq", None),
            P(("rep", "shard"), "seq", None),
            P(("seq", "shard")),
            P(("seq", "shard"), None),
            P(("seq", "shard"), None),
            P(("seq", "shard"), None),
            P(("seq", "shard"), None),
            P(("seq", "shard")),
            P(),
            P(("seq", "shard")),
            P(("seq", "shard"), None),
            P(("rep", "shard"), "seq", None),
            P(("seq", "shard"), "rep", None),
            P(("seq", "shard"), "rep", None),
        ),
        out_specs=(
            P(("rep", "shard"), "seq", None),
            P(("rep", "shard"), "seq", None),
            P(("seq", "shard")),
            P(("seq", "shard"), None),
            P(("seq", "shard"), None),
            P(("seq", "shard"), None),
            P(("seq", "shard"), None),
            P(("seq", "shard")),
            P(("seq", "shard")),
            P(("seq", "shard"), None),
            P(("seq", "shard"), "rep", None),
            P(("seq", "shard"), "rep", None),
        ),
        check_vma=False,
    )
```

```python
from functools import partial

import jax
import jax.numpy as jnp
from jax import lax
from jax.experimental import pallas as pl
from jax.experimental.pallas import tpu as pltpu
from jax.sharding import PartitionSpec as P

BUCKETS = 32
EPSILON = 1e-06
TILE = 128
VMEM_BYTES = 48 * 1024 * 1024
BF16 = jnp.bfloat16
F32 = jnp.float32


def dot_nn(left, right):
    return jnp.dot(left, right, preferred_element_type=F32)


def dot_nt(left, right):
    return lax.dot_general(left, right, (((1,), (1,)), ((), ())), preferred_element_type=F32)


def dot_tn(left, right):
    return lax.dot_general(left, right, (((0,), (0,)), ((), ())), preferred_element_type=F32)


def skew_bias(offset_ref, skewed_ref):
    heads, width = skewed_ref.shape[0], skewed_ref.shape[2]
    row = lax.broadcasted_iota(jnp.int32, (8, width), 0)
    for head in range(heads):
        base = jnp.broadcast_to(offset_ref[head : head + 1, :], (8, width))
        part = pltpu.roll(base, width - (TILE - 1), axis=1)
        for bit in (1, 2, 4):
            part = jnp.where((row & bit) != 0, pltpu.roll(part, bit, axis=1), part)
        for step in (8, 16, 32, 64):
            part = jnp.concatenate([part, pltpu.roll(part, step, axis=1)], axis=0)
        skewed_ref[head] = part


def forward_kernel(
    heads, head_size, row_count, tokens_ref, gain_ref, weight_ref, offset_ref,
    normed_ref, qkv_ref, probs_ref, context_ref, parts, skewed_ref,
):
    block = pl.program_id(0)
    length = tokens_ref.shape[0]
    tiles = length // TILE
    width = heads * head_size

    @pl.when(block == 0)
    def _():
        skew_bias(offset_ref, skewed_ref)
        values = tokens_ref[...].astype(F32)
        scale = lax.rsqrt(jnp.mean(values * values, axis=-1, keepdims=True) + EPSILON)
        normed = (values * scale * gain_ref[...]).astype(BF16)
        normed_ref[...] = normed
        for kind in range(3):
            made = dot_nn(normed, weight_ref[kind]).astype(BF16)
            qkv_ref[kind] = made
            for head in range(heads):
                parts[kind * heads + head] = made[:, head * head_size : (head + 1) * head_size]

    first = pl.multiple_of(block * row_count, row_count)
    contexts = []
    for head in range(heads):
        query = parts[head, pl.ds(first, row_count), :]
        scores = dot_nt(query, parts[heads + head])
        biases = []
        for piece in range(row_count // TILE):
            at = (tiles - 1 - piece - block * (row_count // TILE)) * TILE
            biases.append(skewed_ref[head, :, pl.ds(pl.multiple_of(at, TILE), length)])
        scores = scores + jnp.concatenate(biases, axis=0)
        peak = jnp.max(scores, axis=-1, keepdims=True)
        raised = jnp.exp(scores - peak)
        total = jnp.sum(raised, axis=-1, keepdims=True)
        probs = (raised * (1.0 / total)).astype(BF16)
        probs_ref[head] = probs
        contexts.append(dot_nn(probs, parts[2 * heads + head]))
    context_ref[...] = jnp.concatenate(contexts, axis=1).astype(BF16)


def attention_forward(tokens, gain, weight, offset_bias, heads, head_size):
    length, model_width = tokens.shape
    rows = 512
    width = heads * head_size
    return pl.pallas_call(
        partial(forward_kernel, heads, head_size, rows),
        grid=(length // rows,),
        in_specs=[
            pl.BlockSpec((length, model_width), lambda i: (0, 0)),
            pl.BlockSpec((1, model_width), lambda i: (0, 0)),
            pl.BlockSpec((3, model_width, width), lambda i: (0, 0, 0)),
            pl.BlockSpec(offset_bias.shape, lambda i: (0, 0)),
        ],
        out_specs=[
            pl.BlockSpec((length, model_width), lambda i: (0, 0)),
            pl.BlockSpec((3, length, width), lambda i: (0, 0, 0)),
            pl.BlockSpec((heads, rows, length), lambda i: (0, i, 0)),
            pl.BlockSpec((rows, width), lambda i: (i, 0)),
        ],
        out_shape=[
            jax.ShapeDtypeStruct((length, model_width), BF16),
            jax.ShapeDtypeStruct((3, length, width), BF16),
            jax.ShapeDtypeStruct((heads, length, length), BF16),
            jax.ShapeDtypeStruct((length, width), BF16),
        ],
        scratch_shapes=[
            pltpu.VMEM((3 * heads, length, head_size), BF16),
            pltpu.VMEM((heads, TILE, 2 * length), F32),
        ],
        compiler_params=pltpu.CompilerParams(vmem_limit_bytes=VMEM_BYTES),
        cost_estimate=pl.CostEstimate(
            flops=2 * length * model_width * 3 * width + 4 * length * length * width,
            bytes_accessed=16 * 1024 * 1024,
            transcendentals=heads * length * length,
        ),
    )(tokens, gain, weight, offset_bias)


def backward_kernel(
    heads, head_size, row_count,
    place_ref, qkv_ref, probs_ref, grad_ref, weight_ref, tokens_ref, normed_ref,
    context_ref, out_grad_ref, packed_ref, token_grad_ref, gain_grad_ref, offset_ref,
    parts, dqueries, dkeys, dvalues, diagonals,
):
    block = pl.program_id(0)
    length = qkv_ref.shape[1]
    tiles = length // TILE
    span = diagonals.shape[2]

    @pl.when(block == 0)
    def _():
        for kind in range(3):
            made = qkv_ref[kind]
            for head in range(heads):
                parts[kind * heads + head] = made[:, head * head_size : (head + 1) * head_size]
        shards, reps, seqs, rows, lanes = packed_ref.shape
        shard_rows = normed_ref.shape[1] // (seqs * shards)
        slice_rows = rows - shard_rows
        for rep in range(3 * shard_rows // slice_rows, reps):
            packed_ref[:, rep] = jnp.zeros((shards, seqs, rows, lanes), BF16)
        output_grad = dot_tn(context_ref[...], out_grad_ref[...]).astype(BF16)
        for rep in range(reps):
            columns = output_grad[:, rep * lanes : (rep + 1) * lanes]
            for owner in range(seqs * shards):
                relative = lax.rem(owner % shards + shards - place_ref[0], shards)
                packed_ref[relative, rep, owner // shards, slice_rows:] = columns[
                    owner * shard_rows : (owner + 1) * shard_rows
                ]
        dkeys[...] = jnp.zeros_like(dkeys)
        dvalues[...] = jnp.zeros_like(dvalues)
        diagonals[...] = jnp.zeros_like(diagonals)

    first = pl.multiple_of(block * row_count, row_count)
    grads = grad_ref[...]
    made_queries = []
    for head in range(heads):
        query = parts[head, pl.ds(first, row_count), :]
        grad = grads[:, head * head_size : (head + 1) * head_size]
        probs_low = probs_ref[head]
        probs = probs_low.astype(F32)
        dprobs = dot_nt(grad, parts[2 * heads + head])
        delta = jnp.sum(dprobs * probs, axis=-1, keepdims=True)
        dscores = probs * (dprobs - delta)
        for piece in range(row_count // TILE):
            at = (tiles - 1 - piece - block * (row_count // TILE)) * TILE
            window = pl.ds(pl.multiple_of(at, TILE), length)
            diagonals[head, :, window] += dscores[piece * TILE : (piece + 1) * TILE]
        dscores_low = dscores.astype(BF16)
        made_queries.append(dot_nn(dscores_low, parts[heads + head]))
        dkeys[head] += dot_tn(query, dscores_low)
        dvalues[head] += dot_tn(grad, probs_low)
    dqueries[pl.ds(first, row_count), :] = jnp.concatenate(made_queries, axis=1).astype(BF16)

    @pl.when(block == pl.num_programs(0) - 1)
    def _():
        key_side = jnp.concatenate([dkeys[head] for head in range(heads)], axis=0)
        value_side = jnp.concatenate([dvalues[head] for head in range(heads)], axis=0)
        sides = (dqueries[...], key_side.T.astype(BF16), value_side.T.astype(BF16))
        shards, reps, seqs, rows, lanes = packed_ref.shape
        shard_rows = normed_ref.shape[1] // (seqs * shards)
        slice_rows = rows - shard_rows
        normed = normed_ref[...]
        token_grad = jnp.zeros(tokens_ref.shape, F32)
        for kind in range(3):
            weight_grad = dot_tn(normed, sides[kind]).astype(BF16)
            for owner in range(seqs * shards):
                relative = lax.rem(owner % shards + shards - place_ref[0], shards)
                at = kind * shard_rows
                stop = at + shard_rows
                while at < stop:
                    until = min(stop, (at // slice_rows + 1) * slice_rows)
                    source = owner * shard_rows + at - kind * shard_rows
                    packed_ref[
                        relative,
                        at // slice_rows,
                        owner // shards,
                        at % slice_rows : at % slice_rows + until - at,
                    ] = weight_grad[source : source + until - at]
                    at = until
            token_grad = token_grad + dot_nt(sides[kind], weight_ref[kind])
        token_grad_ref[...] = token_grad.astype(BF16)
        values = tokens_ref[...].astype(F32)
        scale = lax.rsqrt(jnp.mean(values * values, axis=-1, keepdims=True) + EPSILON)
        gain_grad_ref[...] = jnp.sum(token_grad * values * scale, axis=0, keepdims=True)
        row = lax.broadcasted_iota(jnp.int32, (8, span), 0)
        offset_ref[...] = jnp.zeros_like(offset_ref)
        for head in range(heads):
            part = diagonals[head]
            for step in (64, 32, 16, 8):
                part = part[:step] + pltpu.roll(part[step:], span - step, axis=1)
            for bit in (1, 2, 4):
                part = jnp.where((row & bit) != 0, pltpu.roll(part, span - bit, axis=1), part)
            part = pltpu.roll(part, TILE - 1, axis=1)
            offset_ref[head : head + 1, :] = jnp.sum(part, axis=0, keepdims=True)


def attention_backward(
    place, qkv, probs, grad, weight, tokens, normed, context, out_grad,
    heads, head_size, packed_shape,
):
    length, model_width = tokens.shape
    rows = 512
    width = heads * head_size
    padded_heads = -(-heads // 8) * 8
    return pl.pallas_call(
        partial(backward_kernel, heads, head_size, rows),
        grid=(length // rows,),
        in_specs=[
            pl.BlockSpec(memory_space=pltpu.SMEM),
            pl.BlockSpec((3, length, width), lambda i: (0, 0, 0)),
            pl.BlockSpec((heads, rows, length), lambda i: (0, i, 0)),
            pl.BlockSpec((rows, width), lambda i: (i, 0)),
            pl.BlockSpec((3, model_width, width), lambda i: (0, 0, 0)),
            pl.BlockSpec((length, model_width), lambda i: (0, 0)),
            pl.BlockSpec((length, model_width), lambda i: (0, 0)),
            pl.BlockSpec(context.shape, lambda i: (0, 0)),
            pl.BlockSpec(context.shape, lambda i: (0, 0)),
        ],
        out_specs=[
            pl.BlockSpec(packed_shape, lambda i: (0, 0, 0, 0, 0)),
            pl.BlockSpec((length, model_width), lambda i: (0, 0)),
            pl.BlockSpec((1, model_width), lambda i: (0, 0)),
            pl.BlockSpec((padded_heads, 2 * length), lambda i: (0, 0)),
        ],
        out_shape=[
            jax.ShapeDtypeStruct(packed_shape, BF16),
            jax.ShapeDtypeStruct((length, model_width), BF16),
            jax.ShapeDtypeStruct((1, model_width), F32),
            jax.ShapeDtypeStruct((padded_heads, 2 * length), F32),
        ],
        scratch_shapes=[
            pltpu.VMEM((3 * heads, length, head_size), BF16),
            pltpu.VMEM((length, width), BF16),
            pltpu.VMEM((heads, head_size, length), F32),
            pltpu.VMEM((heads, head_size, length), F32),
            pltpu.VMEM((heads, TILE, 2 * length), F32),
        ],
        compiler_params=pltpu.CompilerParams(vmem_limit_bytes=VMEM_BYTES),
        cost_estimate=pl.CostEstimate(
            flops=8 * length * length * width + 12 * length * model_width * width,
            bytes_accessed=16 * 1024 * 1024,
            transcendentals=0,
        ),
    )(place, qkv, probs, grad, weight, tokens, normed, context, out_grad)


def expert_kernel(
    experts, rows_ref, grads_ref, router_ref, picked_ref, up_ref, down_ref,
    weights_grad_ref, rows_grad_ref, returned_ref, logit_grad_ref,
    out_total, in_total, router_probs, low_grads_ref,
):
    step = pl.program_id(0)
    picked = picked_ref[...]

    @pl.when(step == 0)
    def _():
        logits = dot_nn(rows_ref[...], router_ref[...])
        lane = lax.broadcasted_iota(jnp.int32, logits.shape, 1)
        peak = jnp.max(jnp.where(lane < experts, logits, -jnp.inf), axis=-1, keepdims=True)
        raised = jnp.where(lane < experts, jnp.exp(jnp.minimum(logits - peak, 0.0)), 0.0)
        probs = raised / jnp.sum(raised, axis=-1, keepdims=True)
        router_probs[...] = probs
        gate = jnp.sum(probs * picked, axis=-1, keepdims=True)
        low_grads_ref[...] = (gate * grads_ref[...].astype(F32)).astype(BF16)
        out_total[...] = jnp.zeros_like(out_total)
        in_total[...] = jnp.zeros_like(in_total)

    up = up_ref[...]
    down = down_ref[...]
    pre = dot_nt(rows_ref[...], up)
    hidden_grad = dot_nt(low_grads_ref[...], down)
    slope = 0.7978845608028654
    square = pre * pre
    curve = jnp.tanh(slope * pre * (1.0 + 0.044715 * square))
    half = 0.5 * (1.0 + curve)
    hidden = (pre * half).astype(BF16)
    derivative = half + (0.5 * slope) * pre * (1.0 - curve * curve) * (
        1.0 + (3.0 * 0.044715) * square
    )
    pre_grad = (hidden_grad * derivative).astype(BF16)
    weights_grad_ref[0] = dot_tn(pre_grad, rows_ref[...]).astype(BF16)
    weights_grad_ref[1] = dot_tn(hidden, low_grads_ref[...]).astype(BF16)
    out_total[...] += dot_nn(hidden, down)
    in_total[...] += dot_nn(pre_grad, up)

    @pl.when(step == pl.num_programs(0) - 1)
    def _():
        probs = router_probs[...]
        gate = jnp.sum(probs * picked, axis=-1, keepdims=True)
        out = out_total[...].astype(BF16).astype(F32)
        gate_grad = jnp.sum(grads_ref[...].astype(F32) * out, axis=-1, keepdims=True)
        logit_grad = (gate_grad * gate * (picked - probs)).astype(BF16)
        logit_grad_ref[...] = logit_grad
        rows_grad_ref[...] = (in_total[...] + dot_nt(logit_grad, router_ref[...])).astype(BF16)
        returned_ref[...] = (gate * out).astype(BF16)


def expert_pass(rows, grads, router, picked, up, down, experts):
    count, model_width = rows.shape
    units = up.shape[0]
    lanes = router.shape[1]
    block = 1024
    whole = pl.BlockSpec((count, model_width), lambda i: (0, 0))
    return pl.pallas_call(
        partial(expert_kernel, experts),
        grid=(units // block,),
        in_specs=[
            whole,
            whole,
            pl.BlockSpec((model_width, lanes), lambda i: (0, 0)),
            pl.BlockSpec((1, lanes), lambda i: (0, 0)),
            pl.BlockSpec((block, model_width), lambda i: (i, 0)),
            pl.BlockSpec((block, model_width), lambda i: (i, 0)),
        ],
        out_specs=[
            pl.BlockSpec((2, block, model_width), lambda i: (0, i, 0)),
            whole,
            whole,
            pl.BlockSpec((count, lanes), lambda i: (0, 0)),
        ],
        out_shape=[
            jax.ShapeDtypeStruct((2, units, model_width), BF16),
            jax.ShapeDtypeStruct((count, model_width), BF16),
            jax.ShapeDtypeStruct((count, model_width), BF16),
            jax.ShapeDtypeStruct((count, lanes), BF16),
        ],
        scratch_shapes=[
            pltpu.VMEM((count, model_width), F32),
            pltpu.VMEM((count, model_width), F32),
            pltpu.VMEM((count, lanes), F32),
            pltpu.VMEM((count, model_width), BF16),
        ],
        compiler_params=pltpu.CompilerParams(vmem_limit_bytes=VMEM_BYTES),
        cost_estimate=pl.CostEstimate(
            flops=12 * count * units * model_width,
            bytes_accessed=16 * 1024 * 1024,
            transcendentals=count * units,
        ),
    )(rows, grads, router, picked, up, down)


def inverse_rms(values):
    return lax.rsqrt(jnp.mean(values * values, axis=-1, keepdims=True) + EPSILON)


def norm_backward(values, inverse, gain, grad):
    scaled = grad * gain
    return inverse * scaled - values * (
        inverse * inverse * inverse * jnp.mean(scaled * values, axis=-1, keepdims=True)
    )


def gather_rows(rows, axis_name):
    count = lax.axis_size(axis_name)
    place = lax.axis_index(axis_name)
    height = rows.shape[0]
    whole = jnp.zeros((count * height,) + rows.shape[1:], rows.dtype)
    whole = lax.dynamic_update_slice_in_dim(whole, rows, place * height, 0)
    for shift in range(1, count):
        moved = lax.ppermute(rows, axis_name, [(j, (j + shift) % count) for j in range(count)])
        origin = lax.rem(place + count - shift, count)
        whole = lax.dynamic_update_slice_in_dim(whole, moved, origin * height, 0)
    return whole


def reduce_rows(parts, axis_name):
    count = lax.axis_size(axis_name)
    place = lax.axis_index(axis_name)
    total = lax.dynamic_index_in_dim(parts, place, 0, False).astype(F32)
    for shift in range(1, count):
        target = lax.rem(place + shift, count)
        moved = lax.ppermute(
            lax.dynamic_index_in_dim(parts, target, 0, False).astype(BF16),
            axis_name,
            [(j, (j + shift) % count) for j in range(count)],
        )
        total = total + moved.astype(F32)
    return total


def exchange_by_permutes(piece_for, axis_name):
    count = lax.axis_size(axis_name)
    place = lax.axis_index(axis_name)
    held = [piece_for(place)]
    for shift in range(1, count):
        held.append(
            lax.ppermute(
                piece_for(lax.rem(place + shift, count)),
                axis_name,
                [(j, (j + shift) % count) for j in range(count)],
            )
        )
    return [
        lax.select_n(lax.rem(place + count - origin, count), *held) for origin in range(count)
    ]


def after(value, *earlier):
    return lax.optimization_barrier((value,) + earlier)[0]


def exchange(parts, axis_name):
    return lax.all_to_all(parts, axis_name, split_axis=0, concat_axis=0, tiled=True)


def per_device(
    tokens,
    out_grad,
    attention_gain,
    query_weight,
    key_weight,
    value_weight,
    output_weight,
    position_bias,
    bucket_table,
    feedforward_gain,
    router_matrix,
    routes,
    up_weight,
    down_weight,
):
    group = ("seq", "shard")
    seq_count = lax.axis_size("seq")
    shard_count = lax.axis_size("shard")
    rep_count = lax.axis_size("rep")
    seq_place = lax.axis_index("seq")
    owner_count = seq_count * shard_count
    seg_rows = tokens.shape[1]
    model_width = tokens.shape[2]
    length = seg_rows * seq_count
    head_count = position_bias.shape[0] * owner_count // BUCKETS
    head_size = model_width // head_count
    heads = head_count // seq_count
    width = heads * head_size
    experts = router_matrix.shape[1]
    capacity = 2 * seg_rows // experts
    shard_rows = query_weight.shape[0]

    token_rows = tokens[0]
    grad_rows = out_grad[0]

    small = jnp.concatenate(
        [attention_gain, feedforward_gain, position_bias, router_matrix.reshape(-1)]
    )
    small_size = small.shape[0]
    step_rows = 16 * rep_count
    part_rows = -(-(3 * shard_rows + -(-small_size // width)) // step_rows) * step_rows
    small_rows = part_rows - 3 * shard_rows
    small = jnp.pad(small, (0, small_rows * width - small_size)).reshape(small_rows, width)
    whole_tokens = gather_rows(token_rows, "seq")
    quarter = model_width // rep_count
    slice_rows = part_rows // rep_count
    rep_place = lax.axis_index("rep")
    stacked = jnp.concatenate(
        [query_weight, key_weight, value_weight, jnp.tile(small, (1, seq_count))], axis=0
    )
    stacked = lax.dynamic_slice_in_dim(stacked, rep_place * slice_rows, slice_rows, 0)
    output_columns = lax.dynamic_slice_in_dim(output_weight, rep_place * quarter, quarter, 1)
    output_columns = output_columns.reshape(-1, width)

    stacked = stacked.reshape(slice_rows, seq_count, width).transpose(1, 0, 2)
    output_columns = jnp.broadcast_to(
        output_columns[None], (seq_count,) + output_columns.shape
    )
    seq_packed = exchange(jnp.concatenate([stacked, output_columns], axis=1), "seq")
    rep_packed = exchange(
        jnp.broadcast_to(seq_packed[None], (rep_count,) + seq_packed.shape), "rep"
    )
    packed = jnp.stack(exchange_by_permutes(lambda target: rep_packed, "shard"))
    parts = packed[:, :, :, :slice_rows].transpose(2, 0, 1, 3, 4)
    parts = parts.reshape(seq_count, shard_count, part_rows, width)
    qkv_weight = parts[:, :, : 3 * shard_rows].reshape(
        seq_count, shard_count, 3, shard_rows, width
    )
    qkv_weight = qkv_weight.transpose(2, 0, 1, 3, 4).reshape(3, model_width, width)
    small_all = parts[:, :, 3 * shard_rows :].reshape(owner_count, -1)
    output_all = packed[:, :, :, slice_rows:].reshape(
        shard_count, rep_count, seq_count, shard_rows, quarter
    )
    output_all = output_all.transpose(2, 0, 3, 1, 4).reshape(model_width, model_width)
    at = 0
    pieces = []
    for size in (shard_rows, shard_rows, position_bias.shape[0], router_matrix.size):
        pieces.append(small_all[:, at : at + size].reshape(-1))
        at += size
    gain_a = pieces[0].astype(F32)[None]
    gain_f = pieces[1].astype(F32)[None]
    bias_table = pieces[2].reshape(BUCKETS, head_count)
    full_router = pieces[3].reshape(model_width, experts)

    chosen = routes[0, :, 0]
    route_marks = (chosen[:, None] == jnp.arange(experts, dtype=jnp.int32)[None, :]).astype(
        jnp.int32
    )
    slot_ranks = jnp.sum((jnp.cumsum(route_marks, axis=0) - route_marks) * route_marks, axis=-1)
    slot_index = chosen * capacity + slot_ranks
    slots = experts * capacity
    place_marks = (
        slot_index[None, :] == jnp.arange(slots, dtype=jnp.int32)[:, None]
    ).astype(BF16)

    def place_rows(rows):
        return dot_nn(place_marks, rows).astype(BF16)

    def dispatch(placed):
        arrived = exchange(placed.reshape(experts, capacity, model_width), group)
        return arrived.reshape(slots, model_width)

    def send_back(rows):
        back = exchange(rows.reshape(experts, capacity, model_width), group)
        return back.reshape(slots, model_width)

    up_full = lax.all_gather(up_weight, "rep", axis=1, tiled=True)[0]
    down_full = lax.all_gather(down_weight, "rep", axis=1, tiled=True)[0]

    bucket_marks = (
        jnp.pad(bucket_table, (0, 1), constant_values=-1)[None, :]
        == jnp.arange(BUCKETS, dtype=jnp.int32)[:, None]
    ).astype(BF16)
    own_table = lax.dynamic_slice_in_dim(bias_table, seq_place * heads, heads, 1)
    padded_heads = -(-heads // 8) * 8
    own_table = jnp.pad(own_table, ((0, 0), (0, padded_heads - heads)))
    offset_bias = dot_tn(own_table, bucket_marks)

    placed_grads = place_rows(grad_rows)
    whole_tokens, offset_bias, qkv_weight, placed_grads = lax.optimization_barrier(
        (whole_tokens, offset_bias, qkv_weight, placed_grads)
    )
    expert_grads = dispatch(placed_grads)

    normed_whole, qkv, probs, context_own = attention_forward(
        whole_tokens, gain_a, qkv_weight, offset_bias, heads, head_size
    )
    context_own = after(context_own, expert_grads)
    context = exchange(context_own.reshape(seq_count, seg_rows, width), "seq")
    context = context.transpose(1, 0, 2).reshape(seg_rows, model_width)
    inputs = token_rows.astype(F32)
    grads_out = grad_rows.astype(F32)
    middle = inputs + dot_nn(context, output_all)
    middle_inverse = inverse_rms(middle)
    normed_ffn = (middle * middle_inverse * gain_f).astype(BF16)

    expert_rows = dispatch(place_rows(normed_ffn))
    owner = seq_place * shard_count + lax.axis_index("shard")
    lanes = -(-experts // TILE) * TILE
    router_lanes = jnp.pad(full_router, ((0, 0), (0, lanes - experts)))
    picked = (jnp.arange(lanes, dtype=jnp.int32) == owner).astype(F32)[None]
    expert_weights_grad, rows_grad, gated_out, logit_grad = expert_pass(
        expert_rows, expert_grads, router_lanes, picked, up_full, down_full, experts
    )
    grad_back = send_back(rows_grad)
    router_grad = dot_tn(expert_rows, logit_grad)[:, :experts].reshape(owner_count, -1)
    grad_back, router_grad = lax.optimization_barrier((grad_back, router_grad))
    normed_ffn_grad = dot_tn(place_marks, grad_back)
    expert_weights_grad = lax.psum_scatter(
        expert_weights_grad, "rep", scatter_dimension=1, tiled=True
    ).astype(F32)

    gain_f_grad = jnp.sum(normed_ffn_grad * middle * middle_inverse, axis=0)
    middle_grad = grads_out + norm_backward(middle, middle_inverse, gain_f, normed_ffn_grad)
    attn_out_grad = middle_grad.astype(BF16)
    context_grad = dot_nt(attn_out_grad, output_all).astype(BF16)
    context_grad = context_grad.reshape(seg_rows, seq_count, width).transpose(1, 0, 2)
    context_grad = exchange(context_grad, "seq").reshape(length, width)
    returned = send_back(after(gated_out, context_grad))

    shard_place = lax.axis_index("shard").astype(jnp.int32)
    packed_shape = (shard_count, rep_count, seq_count, slice_rows + shard_rows, width)
    weight_parts, normed_grad_part, gain_a_grad, offset_grad = attention_backward(
        shard_place.reshape(1), qkv, probs, context_grad, qkv_weight, whole_tokens, normed_whole,
        context, attn_out_grad, heads, head_size, packed_shape,
    )
    normed_grad_part = after(normed_grad_part, returned)
    weight_parts = after(weight_parts, returned)
    layer_output = (middle + dot_tn(place_marks, returned)).astype(BF16)
    own_table_grad = lax.dot_general(
        bucket_marks.astype(F32),
        offset_grad,
        (((1,), (1,)), ((), ())),
        precision=lax.Precision.HIGHEST,
        preferred_element_type=F32,
    )
    table_grad = lax.dynamic_update_slice_in_dim(
        jnp.zeros((BUCKETS, head_count), F32), own_table_grad[:, :heads], seq_place * heads, 1
    )

    normed_grad = reduce_rows(
        normed_grad_part.reshape(seq_count, seg_rows, model_width), "seq"
    )

    small_grad = jnp.concatenate(
        [
            gain_a_grad.reshape(owner_count, -1),
            gain_f_grad.reshape(owner_count, -1),
            table_grad.reshape(owner_count, -1),
            router_grad,
        ],
        axis=1,
    )
    small_grad = jnp.pad(small_grad, ((0, 0), (0, small_rows * width - small_size)))
    small_grad = small_grad.reshape(seq_count, shard_count, small_rows, width)
    small_grad = small_grad.transpose(1, 0, 2, 3).astype(BF16)[:, None]
    small_grad = jnp.stack(
        [
            lax.dynamic_index_in_dim(
                small_grad, lax.rem(shard_place + shift, shard_count), 0, False
            )
            for shift in range(shard_count)
        ]
    )
    at = 3 * shard_rows
    while at < part_rows:
        until = min(part_rows, (at // slice_rows + 1) * slice_rows)
        weight_parts = lax.dynamic_update_slice(
            weight_parts,
            small_grad[:, :, :, at - 3 * shard_rows : until - 3 * shard_rows],
            (0, at // slice_rows, 0, at % slice_rows, 0),
        )
        at = until
    shard_total = weight_parts[0].astype(F32)
    for shift in range(1, shard_count):
        shard_total = shard_total + lax.ppermute(
            weight_parts[shift],
            "shard",
            [(j, (j + shift) % shard_count) for j in range(shard_count)],
        ).astype(F32)
    weight_parts = shard_total.astype(BF16)
    weight_parts = reduce_rows(weight_parts, "rep").astype(BF16)
    weight_parts, normed_grad = lax.optimization_barrier((weight_parts, normed_grad))
    weight_parts = exchange_by_permutes(
        lambda target: lax.dynamic_index_in_dim(weight_parts, target, 0, False), "seq"
    )
    token_inverse = inverse_rms(inputs)
    token_input_gradient = middle_grad + norm_backward(inputs, token_inverse, gain_a, normed_grad)

    output_part = sum(part[slice_rows:].astype(F32) for part in weight_parts).astype(BF16)
    slices = jnp.concatenate([part[:slice_rows] for part in weight_parts] + [output_part], axis=0)
    slices = exchange_by_permutes(lambda target: slices, "rep")
    weight_rows = jnp.concatenate(
        [
            jnp.concatenate(
                [
                    part[origin * slice_rows : (origin + 1) * slice_rows]
                    for origin in range(seq_count)
                ],
                axis=1,
            )
            for part in slices
        ],
        axis=0,
    ).astype(F32)
    matrices = [weight_rows[k * shard_rows : (k + 1) * shard_rows] for k in range(3)]
    output_slices = [
        part[seq_count * slice_rows :].reshape(shard_rows, quarter) for part in slices
    ]
    matrices.append(jnp.concatenate(output_slices, axis=1).astype(F32))
    smalls = weight_rows[3 * shard_rows :].reshape(small_rows, seq_count, width)
    smalls = jnp.sum(smalls, axis=1).reshape(-1)[:small_size]
    table_size = position_bias.shape[0]
    return (
        layer_output[None],
        token_input_gradient[None],
        smalls[:shard_rows],
        matrices[0],
        matrices[1],
        matrices[2],
        matrices[3],
        smalls[2 * shard_rows : 2 * shard_rows + table_size],
        smalls[shard_rows : 2 * shard_rows],
        smalls[2 * shard_rows + table_size :].reshape(shard_rows, experts),
        expert_weights_grad[:1],
        expert_weights_grad[1:],
    )


def solution(mesh):
    return jax.shard_map(
        per_device,
        mesh=mesh,
        in_specs=(
            P(("rep", "shard"), "seq", None),
            P(("rep", "shard"), "seq", None),
            P(("seq", "shard")),
            P(("seq", "shard"), None),
            P(("seq", "shard"), None),
            P(("seq", "shard"), None),
            P(("seq", "shard"), None),
            P(("seq", "shard")),
            P(),
            P(("seq", "shard")),
            P(("seq", "shard"), None),
            P(("rep", "shard"), "seq", None),
            P(("seq", "shard"), "rep", None),
            P(("seq", "shard"), "rep", None),
        ),
        out_specs=(
            P(("rep", "shard"), "seq", None),
            P(("rep", "shard"), "seq", None),
            P(("seq", "shard")),
            P(("seq", "shard"), None),
            P(("seq", "shard"), None),
            P(("seq", "shard"), None),
            P(("seq", "shard"), None),
            P(("seq", "shard")),
            P(("seq", "shard")),
            P(("seq", "shard"), None),
            P(("seq", "shard"), "rep", None),
            P(("seq", "shard"), "rep", None),
        ),
        check_vma=False,
    )
```
